128 devices in a mesh: qrow: 16 (over x, z_hi, core), kvcol: 8 (over y, z_lo).
Axes of the slice: x: 4, y: 4, z: 4 (z_hi: 2, z_lo: 2; z = z_hi * 2 + z_lo), core: 2. Of those that a mesh axis runs over, the one named last changes fastest.
Arguments:
- queries: bfloat16 [8, 2048, 4096], P('kvcol', 'qrow'), may hold values from -90 to 90, as said below
- shared_kv: bfloat16 [2, 16, 1024, 512], P(None, 'qrow', 'kvcol'), may hold values from -16 to 16, as said below
- document: int32 [16384], P(('qrow', 'kvcol')), may hold values from 0 to 16777215, as said below
Outputs:
- attended: bfloat16 [8, 2048, 4096], P('kvcol', 'qrow')
The draws below stay inside these ranges and needn't reach their ends.
Inputs may be any that keep to these rules, and one draw needn't show every extreme that they name: Document labels never fall along the tokens and differ between documents; each document holds 1 to 8192 tokens, one exactly that many. `queries`: real numbers within the stated range. `shared_kv`: real numbers within the stated range.
All inputs are finite; a program needn't handle non-finite values.
Results may differ from the reference program's by a relative error of at most 0.017.
Values may be sent and summed in bfloat16 or wider, within the bound.
A program may use at most 256 MiB of HBM per device.

```python
import jax
import jax.numpy as jnp
from jax import lax

HEAD = 128
Q_HEADS = 16
KV_HEADS = 4
LAYERS = 2
TOKENS = 16384
QCHUNK = 2048
KCHUNK = 1024
QW = 4096
KVW = 512
DOCS = 20
LABELS = 16777216
N_QROW = 16
N_KVCOL = 8


def raw_keys(key):
    return jnp.clip(jax.random.normal(jax.random.fold_in(key, 5), (TOKENS, KVW), jnp.float32), -4.5, 4.5)


def layout(key):
    longest = TOKENS // 2
    rest = TOKENS - longest
    picked = jax.random.choice(jax.random.fold_in(key, 17), rest - 1, (DOCS - 2,), replace=False)
    cuts = jnp.sort(picked.astype(jnp.int32) + 1)
    starts = jnp.concatenate([jnp.zeros((1,), jnp.int32), cuts, jnp.full((1,), rest, jnp.int32)])
    place = jax.random.randint(jax.random.fold_in(key, 18), (), 0, DOCS, dtype=jnp.int32)
    long_start = jnp.take(starts, place)
    positions = jnp.arange(TOKENS, dtype=jnp.int32)
    inside = (positions >= long_start) & (positions < long_start + longest)
    before = positions < long_start
    shifted = jnp.where(before, positions, positions - longest)
    counted = jnp.sum((cuts[None, :] <= shifted[:, None]).astype(jnp.int32), axis=1)
    index = jnp.where(inside, place, jnp.where(before, counted, counted + 1))
    return index


def draw_document(key, part):
    index = layout(key)
    key = jax.random.fold_in(key, 4)
    spacing = (LABELS - 1) // (DOCS - 1)
    offsets = jax.random.randint(key, (DOCS,), 0, spacing, dtype=jnp.int32)
    order = jnp.arange(DOCS, dtype=jnp.int32)
    labels = order * spacing + offsets
    labels = jnp.where(order == 0, 0, labels)
    labels = jnp.where(order == DOCS - 1, LABELS - 1, labels)
    return jnp.take(labels, index).astype(jnp.int32)


def draw_queries(key, part):
    key = jax.random.fold_in(key, 1)
    drawn = jnp.clip(jax.random.normal(key, (TOKENS, QW), jnp.float32), -4.5, 4.5)
    return drawn.reshape(N_KVCOL, QCHUNK, QW).astype(jnp.bfloat16)


def draw_shared_kv(key, part):
    keys = raw_keys(key)
    key = jax.random.fold_in(key, 2)
    values = jnp.clip(jax.random.normal(key, (TOKENS, KVW), jnp.float32), -4.5, 4.5)
    both = jnp.stack([keys, values], axis=0)
    return both.reshape(2, N_QROW, KCHUNK, KVW).astype(jnp.bfloat16)


def setup_inputs(seed: int = 0) -> dict:
    key_list = jax.random.split(jax.random.key(seed), 4)
    queries = draw_queries(jax.random.fold_in(key_list[3], 71), 0)
    shared_kv = draw_shared_kv(jax.random.fold_in(key_list[3], 71), 0)
    document = draw_document(jax.random.fold_in(key_list[3], 71), 0)
    return {"queries": queries, "shared_kv": shared_kv, "document": document}


NEG = -1e30


def tile_terms(qrows, qpos, qdoc, keys, values, kpos, kdoc):
    rows = qrows.shape[0]
    group = Q_HEADS // KV_HEADS
    allowed = (qdoc[:, None] == kdoc[None, :]) & (kpos[None, :] <= qpos[:, None])

    def one_head_group(index):
        which = index % KV_HEADS
        qblock = lax.dynamic_slice_in_dim(qrows, index * group * HEAD, group * HEAD, 1).reshape(rows, group, HEAD)
        kblock = lax.dynamic_slice_in_dim(keys, which * HEAD, HEAD, 1)
        vblock = lax.dynamic_slice_in_dim(values, which * HEAD, HEAD, 1)
        scores = jnp.einsum('rjd,kd->jrk', qblock.astype(jnp.float32), kblock.astype(jnp.float32)) * (HEAD ** -0.5)
        scores = jnp.where(allowed[None], scores, NEG)
        top = jnp.max(scores, axis=2)
        weights = jnp.where(allowed[None], jnp.exp(scores - top[:, :, None]), 0.0)
        total = jnp.sum(weights, axis=2)
        rounded = lax.optimization_barrier(weights.astype(jnp.bfloat16)).astype(jnp.float32)
        mixed = jnp.einsum('jrk,kd->rjd', rounded, vblock.astype(jnp.float32)).reshape(rows, group * HEAD)
        return mixed, total.T, top.T

    mixed, total, top = lax.map(one_head_group, jnp.arange(LAYERS * KV_HEADS, dtype=jnp.int32))
    mixed = jnp.transpose(mixed, (1, 0, 2)).reshape(rows, -1)
    total = jnp.transpose(total, (1, 0, 2)).reshape(rows, -1)
    top = jnp.transpose(top, (1, 0, 2)).reshape(rows, -1)
    return mixed, total, top


def reference(queries, shared_kv, document):
    qall = queries.reshape(TOKENS, QW)
    keys = shared_kv[0].reshape(TOKENS, KVW)
    values = shared_kv[1].reshape(TOKENS, KVW)
    block = 512 if TOKENS % 512 == 0 else TOKENS

    def per_query(index):
        start = index * block
        qrows = lax.dynamic_slice_in_dim(qall, start, block, 0)
        qpos = start + jnp.arange(block, dtype=jnp.int32)
        qdoc = lax.dynamic_slice_in_dim(document, start, block, 0)

        def per_key(kidx):
            kstart = kidx * KCHUNK
            kpos = kstart + jnp.arange(KCHUNK, dtype=jnp.int32)
            return tile_terms(qrows, qpos, qdoc,
                              lax.dynamic_slice_in_dim(keys, kstart, KCHUNK, 0),
                              lax.dynamic_slice_in_dim(values, kstart, KCHUNK, 0),
                              kpos, lax.dynamic_slice_in_dim(document, kstart, KCHUNK, 0))

        mixed, total, top = lax.map(per_key, jnp.arange(N_QROW, dtype=jnp.int32))
        peak = jnp.max(top, axis=0)
        factor = jnp.exp(top - peak[None])
        term = mixed * jnp.repeat(factor, HEAD, axis=2)
        term = lax.optimization_barrier(term.astype(jnp.bfloat16)).astype(jnp.float32)
        numer = jnp.sum(term, axis=0)
        denom = jnp.sum(total * factor, axis=0)
        return (numer / jnp.repeat(denom, HEAD, axis=1)).astype(jnp.bfloat16)

    out = lax.map(per_query, jnp.arange(TOKENS // block, dtype=jnp.int32))
    return out.reshape(N_KVCOL, QCHUNK, QW)
```

```python
import functools
import jax
import jax.numpy as jnp
from jax import lax
from jax.experimental import pallas as pl
from jax.experimental.pallas import tpu as pltpu
from jax.sharding import PartitionSpec as P

HEAD = 128
Q_HEADS = 16
KV_HEADS = 4
LAYERS = 2
GROUP = Q_HEADS // KV_HEADS
TOK = 128
MESH = pl.DeviceIdType.MESH


def place():
    row, col = lax.axis_index("qrow"), lax.axis_index("kvcol")
    return row // 4, col // 2, ((row // 2) % 2) * 2 + col % 2, row % 2


def row_of(x, z, core):
    return (x * 2 + z // 2) * 2 + core


def device(x, y, z, core):
    return (row_of(x, z, core), y * 2 + z % 2)


def greet(devices):
    barrier = pltpu.get_barrier_semaphore()
    for d in devices:
        pl.semaphore_signal(barrier, inc=1, device_id=d, device_id_type=MESH)
    pl.semaphore_wait(barrier, len(devices))


class Copies:
    def __init__(self, send_sem, recv_sem):
        self.send_sem, self.recv_sem, self.started = send_sem, recv_sem, []

    def send(self, src, dst, to):
        n = len(self.started)
        copy = pltpu.make_async_remote_copy(
            src_ref=src, dst_ref=dst, send_sem=self.send_sem.at[n], recv_sem=self.recv_sem.at[n],
            device_id=to, device_id_type=MESH,
        )
        copy.start()
        self.started.append(copy)
        return copy

    def finish(self):
        for copy in self.started:
            copy.wait_send()


GATHER_COPIES = 3 + 6 + 2 * (4 * 2 + 4 + 4 * 2 + 4 * 2) + 32


def gather_kernel(q_ref, kv_ref, qx_ref, kvx_ref, send_sem, recv_sem, here_sem):
    x, y, z, core = place()
    col = lax.axis_index("kvcol")
    row = lax.axis_index("qrow")
    nx = [(x + 1) % 4, (x + 3) % 4]
    nz = [(z + 1) % 4, (z + 3) % 4]
    ys = [(y + k) % 4 for k in range(4)]
    beside = device(x, y, z, 1 - core)
    legs = {0: [device(v, y, z, core) for v in nx], 1: [device(x, y, v, core) for v in nz]}
    greet(legs[0] + legs[1] + [beside] + [device(x, ys[k], z, core) for k in (1, 2, 3)])

    copies = Copies(send_sem, recv_sem)

    def part(half, bx, bz, which):
        return kvx_ref.at[half, row_of(bx, bz, core), which, bz % 2]

    def head_slice(ref, index, width):
        return ref.at[:, pl.ds(pl.multiple_of(index * width, width), width)]

    every = pl.ds(0, 4)
    own = [head_slice(kv_ref.at[h], y, HEAD) for h in (0, 1)]
    local = []
    for h in (0, 1):
        c = pltpu.make_async_copy(own[h], part(h, x, z, y), here_sem.at[h])
        c.start()
        local.append(c)
    first = {}
    for h in (0, 1):
        for way in (0, 1):
            first[h, 0, way] = copies.send(own[h], part(h, x, z, y), legs[h][way])
    across = {}
    for k in (1, 3, 2):
        src = kv_ref.at[:, :, pl.ds(pl.multiple_of(ys[k] * HEAD, HEAD), HEAD)]
        across[k] = copies.send(src, kvx_ref.at[:, row, y, z % 2], device(x, ys[k], z, core))
    width = GROUP * HEAD
    asked = []
    for layer in range(LAYERS):
        c = pltpu.make_async_copy(
            head_slice(q_ref, layer * KV_HEADS + y, width), qx_ref.at[y, layer], here_sem.at[2 + layer])
        c.start()
        local.append(c)
    for k in (1, 3, 2):
        for layer in range(LAYERS):
            asked.append(copies.send(
                head_slice(q_ref, layer * KV_HEADS + ys[k], width), qx_ref.at[y, layer], device(x, ys[k], z, core)))
    for k in (1, 3, 2):
        across[k].wait_recv()
        for h in (0, 1):
            ref = part(h, x, z, (y + 4 - k) % 4)
            for way in (0, 1):
                first[h, k, way] = copies.send(ref, ref, legs[h][way])
    for c in local[:2]:
        c.wait()

    given = []

    def share(half, bx, bz):
        ref = part(half, bx, bz, every)
        given.append(copies.send(ref, ref, beside))

    second = {}

    def onward(half, step, bx, bz):
        ref = part(half, bx, bz, every)
        for way in (0, 1):
            second[half, step, way] = copies.send(ref, ref, legs[1 - half][way])
        share(half, bx, bz)

    def came(half, way):
        if half == 0:
            return (nx[1 - way], z)
        return (x, nz[1 - way])

    for h in (0, 1):
        onward(h, 0, x, z)
    further = {}
    for k in (0, 1, 3, 2):
        way = 0 if k < 2 else 1
        for h in (0, 1):
            first[h, k, way].wait_recv()
            ref = part(h, *came(h, way), (y + 4 - k) % 4)
            further[h, k] = copies.send(ref, ref, legs[h][way])
    for way in (0, 1):
        for k in ((2, 3), (0, 1))[way]:
            for h in (0, 1):
                first[h, k, way].wait_recv()
        for h in (0, 1):
            onward(h, 1 + way, *came(h, way))
    for h in (0, 1):
        for k in range(4):
            further[h, k].wait_recv()
        opposite = ((x + 2) % 4, z) if h == 0 else (x, (z + 2) % 4)
        onward(h, 3, *opposite)

    def row_block(half, step):
        if half == 0:
            return [x, nx[1], nx[0], (x + 2) % 4][step]
        return [z, nz[1], nz[0], (z + 2) % 4][step]

    last = {}
    for step in range(4):
        for h in (0, 1):
            for way in (0, 1):
                second[h, step, way].wait_recv()
                b = row_block(h, step)
                bx, bz = (b, nz[1 - way]) if h == 0 else (nx[1 - way], b)
                ref = part(h, bx, bz, pl.ds(2 * way, 2))
                last[h, step, way] = copies.send(ref, ref, legs[1 - h][way])
                share(h, bx, bz)
    for step in range(4):
        for h in (0, 1):
            for way in (0, 1):
                last[h, step, way].wait_recv()
            b = row_block(h, step)
            share(h, *((b, (z + 2) % 4) if h == 0 else ((x + 2) % 4, b)))
    for c in given:
        c.wait_recv()
    for c in asked:
        c.wait_recv()
    for c in local[2:]:
        c.wait()
    copies.finish()


def gather(q, kv):
    anywhere = pl.BlockSpec(memory_space=pl.ANY)
    return pl.pallas_call(
        gather_kernel,
        out_shape=[
            jax.ShapeDtypeStruct((KV_HEADS, LAYERS, TOK, GROUP * HEAD), q.dtype),
            jax.ShapeDtypeStruct((2, 16, 4, 2, TOK, HEAD), kv.dtype),
        ],
        in_specs=[anywhere] * 2,
        out_specs=[anywhere] * 2,
        scratch_shapes=[
            pltpu.SemaphoreType.DMA((GATHER_COPIES,)),
            pltpu.SemaphoreType.DMA((GATHER_COPIES,)),
            pltpu.SemaphoreType.DMA((4,)),
        ],
        compiler_params=pltpu.CompilerParams(collective_id=0, has_side_effects=True),
    )(q, kv)


def return_kernel(o_ref, out_ref, send_sem, recv_sem, here_sem):
    x, y, z, core = place()
    ys = [(y + k) % 4 for k in range(4)]
    others = [device(x, ys[k], z, core) for k in (1, 3, 2)]
    greet(others)
    copies = Copies(send_sem, recv_sem)
    width = GROUP * HEAD

    def mine(layer):
        return out_ref.at[:, pl.ds(pl.multiple_of((layer * KV_HEADS + y) * width, width), width)]

    for k, to in zip((1, 3, 2), others):
        for layer in range(LAYERS):
            copies.send(o_ref.at[ys[k], layer], mine(layer), to)
    local = [pltpu.make_async_copy(o_ref.at[y, layer], mine(layer), here_sem.at[layer]) for layer in range(LAYERS)]
    for c in local:
        c.start()
    for c in local:
        c.wait()
    for c in copies.started:
        c.wait_recv()
    copies.finish()


def give_back(o):
    anywhere = pl.BlockSpec(memory_space=pl.ANY)
    return pl.pallas_call(
        return_kernel,
        out_shape=jax.ShapeDtypeStruct((TOK, LAYERS * Q_HEADS * HEAD), o.dtype),
        in_specs=[anywhere],
        out_specs=anywhere,
        scratch_shapes=[
            pltpu.SemaphoreType.DMA((6,)),
            pltpu.SemaphoreType.DMA((6,)),
            pltpu.SemaphoreType.DMA((2,)),
        ],
        compiler_params=pltpu.CompilerParams(collective_id=1, has_side_effects=True),
    )(o)


SCALE = 1.4426950408889634 * HEAD ** -0.5
NEG=-1e30
BIG = 100.0
KB = 512

def attend_kernel(kb, rg, start_ref, same_ref, longest_ref, chunk_ref, q_ref, docs_ref, kv_ref, o_ref, k_buf, v_buf, q_buf, acc, top, sem):
    tiles = q_ref.shape[0]
    heads = LAYERS*GROUP
    rows = heads*TOK
    total = kv_ref.shape[1]
    piece = total//tiles
    for i in range(tiles):
        src = pl.ds(i*piece, piece); dst = pl.ds(kb + i*piece, piece)
        pltpu.make_async_copy(kv_ref.at[0, src], k_buf.at[dst], sem.at[0, i]).start()
        pltpu.make_async_copy(kv_ref.at[1, src], v_buf.at[dst], sem.at[1, i]).start()
    k_buf[0:kb] = jnp.zeros((kb, HEAD), k_buf.dtype)
    v_buf[0:kb] = jnp.zeros((kb, HEAD), v_buf.dtype)
    ones = jnp.ones((kb, HEAD), v_buf.dtype)
    sub = kb//TOK

    for t in range(tiles):
        src = pl.ds(t*piece, piece); dst = pl.ds(kb + t*piece, piece)
        for l in range(LAYERS):
            for h in range(GROUP):
                q_buf[pl.ds((l*GROUP+h)*TOK, TOK), :] = q_ref[t, l, :, h*HEAD:(h+1)*HEAD]
        length = jnp.float32(0)
        for g in range(heads):
            qf = q_buf[pl.ds(g*TOK, TOK), :].astype(jnp.float32)
            length = jnp.maximum(length, jnp.max(jnp.sum(qf*qf, axis=1, keepdims=True)))
        small = length*longest_ref[0] <= (BIG/SCALE)**2
        chunk = chunk_ref[t]
        end = (chunk + 1)*TOK
        first = start_ref[t]
        span = end - first
        blocks = (span + kb - 1)//kb
        full = jnp.where(same_ref[t] == 1, jnp.maximum(span//kb, 1), 1)
        qd = jnp.transpose(jnp.broadcast_to(docs_ref[pl.ds(chunk + sub, 1), :], (TOK, TOK)))
        pltpu.make_async_copy(kv_ref.at[0, src], k_buf.at[dst], sem.at[0, t]).wait()
        pltpu.make_async_copy(kv_ref.at[1, src], v_buf.at[dst], sem.at[1, t]).wait()
        acc[...] = jnp.zeros_like(acc)
        tri = lax.broadcasted_iota(jnp.int32, (TOK, TOK), 1) <= lax.broadcasted_iota(jnp.int32, (TOK, TOK), 0)

        def allowed(i):
            parts = []
            base = chunk + 1 - (i+1)*sub + sub
            for s in range(sub):
                kd = docs_ref[pl.ds(base + s, 1), :]
                m = qd == kd
                if s == sub-1:
                    m = m & (tri | (i > 0))
                parts.append(m)
            return jnp.concatenate(parts, axis=1)

        def quick(i, masked):
            at = pl.multiple_of(end - (i+1)*kb + kb, TOK)
            k = k_buf[pl.ds(at, kb), :]
            v = jnp.concatenate([v_buf[pl.ds(at, kb), :], ones], axis=1)
            if masked:
                mask = allowed(i)
            for g in range(rows//rg):
                r = pl.ds(g*rg, rg)
                s = lax.dot_general(q_buf[r, :], k, (((1,),(1,)),((),())), preferred_element_type=jnp.float32)
                p = jnp.exp2(s*SCALE)
                if masked:
                    p = jnp.where(jnp.concatenate([mask]*(rg//TOK), axis=0), p, 0.0)
                acc[r, :] += jnp.dot(p.astype(jnp.bfloat16), v, preferred_element_type=jnp.float32)

        def careful(i, masked):
            at = pl.multiple_of(end - (i+1)*kb + kb, TOK)
            k = k_buf[pl.ds(at, kb), :]
            v = jnp.concatenate([v_buf[pl.ds(at, kb), :], ones], axis=1)
            mask = allowed(i)
            for g in range(rows//TOK):
                r = pl.ds(g*TOK, TOK)
                s = lax.dot_general(q_buf[r, :], k, (((1,),(1,)),((),())), preferred_element_type=jnp.float32)*SCALE
                s = jnp.where(mask, s, NEG)
                old = top[r, :]
                new = jnp.maximum(old, jnp.max(s, axis=1, keepdims=True))
                top[r, :] = new
                p = jnp.where(mask, jnp.exp2(s - new[:, :1]), 0.0)
                keep = jnp.exp2(old - new)
                acc[r, :] = acc[r, :]*jnp.concatenate([keep, keep], axis=1) + jnp.dot(p.astype(jnp.bfloat16), v, preferred_element_type=jnp.float32)

        def at_masked(idx):
            return jnp.where(idx == 0, 0, idx - 1 + full)

        @pl.when(small)
        def _():
            lax.fori_loop(0, 1 + blocks - jnp.minimum(full, blocks), lambda n, _: quick(at_masked(n), True), None)
            lax.fori_loop(1, full, lambda n, _: quick(n, False), None)

        @pl.when(jnp.logical_not(small))
        def _():
            top[...] = jnp.full_like(top, NEG)
            lax.fori_loop(0, blocks, lambda n, _: careful(n, True), None)

        for l in range(LAYERS):
            for h in range(GROUP):
                r = pl.ds((l*GROUP+h)*TOK, TOK)
                a = acc[r, :]
                o_ref[t, l, :, h*HEAD:(h+1)*HEAD] = (a[:, :HEAD]/a[:, HEAD:]).astype(o_ref.dtype)

def attend(start, same, longest, chunk, q, docs, kv, kb=KB, rg=256):
    tiles = q.shape[0]
    rows = LAYERS*GROUP*TOK
    total = kv.shape[1]
    smem = pl.BlockSpec(memory_space=pltpu.SMEM)
    vmem = pl.BlockSpec(memory_space=pltpu.VMEM)
    return pl.pallas_call(
        functools.partial(attend_kernel, kb, rg),
        out_shape=jax.ShapeDtypeStruct(q.shape, q.dtype),
        in_specs=[smem]*4 + [vmem, vmem, pl.BlockSpec(memory_space=pl.ANY)],
        out_specs=vmem,
        scratch_shapes=[
            pltpu.VMEM((kb + total, HEAD), jnp.bfloat16),
            pltpu.VMEM((kb + total, HEAD), jnp.bfloat16),
            pltpu.VMEM((rows, HEAD), jnp.bfloat16),
            pltpu.VMEM((rows, 2*HEAD), jnp.float32),
            pltpu.VMEM((rows, HEAD), jnp.float32),
            pltpu.SemaphoreType.DMA((2, tiles)),
        ],
        compiler_params=pltpu.CompilerParams(vmem_limit_bytes=50*2**20),
    )(start, same, longest, chunk, q, docs, kv)


def shards(queries, shared_kv, document):
    row, col = lax.axis_index("qrow"), lax.axis_index("kvcol")
    mine = col // 2
    q = queries[0]
    kv = shared_kv[:, 0]
    keys = kv[0].astype(jnp.float32).reshape(TOK, KV_HEADS, HEAD)
    longest = jnp.ceil(jnp.max(jnp.sum(keys * keys, axis=2), axis=0)).astype(jnp.int32)
    note = jnp.concatenate([document, longest, jnp.zeros((TOK - KV_HEADS,), jnp.int32)])
    notes = lax.all_gather(note, ("qrow", "kvcol"), axis=0, tiled=False)
    docs = notes[:, :TOK]
    longest = lax.dynamic_slice_in_dim(jnp.max(notes[:, TOK:TOK + KV_HEADS], axis=0), mine, 1, 0).astype(jnp.float32)
    qx, kvx = gather(q, kv)
    kvx = kvx.reshape(2, -1, HEAD)
    chunk = jnp.arange(4, dtype=jnp.int32) * 32 + (col % 2) * 16 + row
    ends = jnp.take(docs[:, ::TOK - 1], chunk, axis=0)
    start = jnp.sum((docs[None] < ends[:, 0, None, None]).astype(jnp.int32), axis=(1, 2))
    same = (ends[:, 0] == ends[:, 1]).astype(jnp.int32)
    padded = jnp.concatenate([jnp.full((KB // TOK, TOK), -1, jnp.int32), docs])
    o = attend(start, same, longest, chunk, qx, padded, kvx)
    out = give_back(o)
    return out.reshape(queries.shape)


def solution(mesh):
    placed = (P("kvcol", "qrow", None), P(None, "qrow", "kvcol", None), P(("qrow", "kvcol")))
    return jax.shard_map(
        shards, mesh=mesh, in_specs=placed, out_specs=P("kvcol", "qrow", None), check_vma=False
    )
```

```python
import functools
import jax
import jax.numpy as jnp
from jax import lax
from jax.experimental import pallas as pl
from jax.experimental.pallas import tpu as pltpu
from jax.sharding import PartitionSpec as P

HEAD = 128
Q_HEADS = 16
KV_HEADS = 4
LAYERS = 2
GROUP = Q_HEADS // KV_HEADS
TOK = 128
MESH = pl.DeviceIdType.MESH


def place():
    row, col = lax.axis_index("qrow"), lax.axis_index("kvcol")
    return row // 4, col // 2, ((row // 2) % 2) * 2 + col % 2, row % 2


def row_of(x, z, core):
    return (x * 2 + z // 2) * 2 + core


def device(x, y, z, core):
    return (row_of(x, z, core), y * 2 + z % 2)


def greet(devices):
    barrier = pltpu.get_barrier_semaphore()
    for d in devices:
        pl.semaphore_signal(barrier, inc=1, device_id=d, device_id_type=MESH)
    pl.semaphore_wait(barrier, len(devices))


class Copies:
    def __init__(self, send_sem, recv_sem):
        self.send_sem, self.recv_sem, self.started = send_sem, recv_sem, []

    def send(self, src, dst, to):
        n = len(self.started)
        copy = pltpu.make_async_remote_copy(
            src_ref=src, dst_ref=dst, send_sem=self.send_sem.at[n], recv_sem=self.recv_sem.at[n],
            device_id=to, device_id_type=MESH,
        )
        copy.start()
        self.started.append(copy)
        return copy

    def finish(self):
        for copy in self.started:
            copy.wait_send()


GATHER_COPIES = 3 + 6 + 2 * (4 * 2 + 4 + 4 * 2 + 4 * 2) + 32 + 10


def gather_kernel(q_ref, kv_ref, doc_ref, qx_ref, kvx_ref, notes_ref, k_buf, note, send_sem, recv_sem, here_sem):
    x, y, z, core = place()
    col = lax.axis_index("kvcol")
    row = lax.axis_index("qrow")
    nx = [(x + 1) % 4, (x + 3) % 4]
    nz = [(z + 1) % 4, (z + 3) % 4]
    ys = [(y + k) % 4 for k in range(4)]
    beside = device(x, y, z, 1 - core)
    legs = {0: [device(v, y, z, core) for v in nx], 1: [device(x, y, v, core) for v in nz]}
    xs = [device((x + k) % 4, y, z, core) for k in (1, 3, 2)]
    zs = [device(x, y, (z + k) % 4, core) for k in (1, 3, 2)]
    greet(xs + zs + [beside] + [device(x, ys[k], z, core) for k in (1, 2, 3)])

    copies = Copies(send_sem, recv_sem)

    def part(half, bx, bz, which):
        return kvx_ref.at[half, row_of(bx, bz, core), which, bz % 2]

    def head_slice(ref, index, width):
        return ref.at[:, pl.ds(pl.multiple_of(index * width, width), width)]

    every = pl.ds(0, 4)
    own = [head_slice(kv_ref.at[h], y, HEAD) for h in (0, 1)]
    local = []
    for h in (0, 1):
        c = pltpu.make_async_copy(own[h], part(h, x, z, y), here_sem.at[h])
        c.start()
        local.append(c)
    first = {}
    for h in (0, 1):
        for way in (0, 1):
            first[h, 0, way] = copies.send(own[h], part(h, x, z, y), legs[h][way])
    across = {}
    for k in (1, 3, 2):
        src = kv_ref.at[:, :, pl.ds(pl.multiple_of(ys[k] * HEAD, HEAD), HEAD)]
        across[k] = copies.send(src, kvx_ref.at[:, row, y, z % 2], device(x, ys[k], z, core))
    c = pltpu.make_async_copy(kv_ref.at[0], k_buf, here_sem.at[4])
    c.start()
    c.wait()
    lane = lax.broadcasted_iota(jnp.int32, (1, TOK), 1)
    lengths = jnp.zeros((1, TOK), jnp.int32)
    for h in range(KV_HEADS):
        k = k_buf[:, h * HEAD:(h + 1) * HEAD].astype(jnp.float32)
        most = jnp.max(jnp.sum(k * k, axis=1, keepdims=True), axis=0, keepdims=True)
        lengths = jnp.where(lane == h, most.astype(jnp.int32) + 1, lengths)
    note[0:1, :] = doc_ref[...]
    note[1:2, :] = lengths
    zh, zl = z // 2, z % 2
    c = pltpu.make_async_copy(note, notes_ref.at[x, zh, core, y, zl], here_sem.at[5])
    c.start()
    local.append(c)
    told = [copies.send(note, notes_ref.at[x, zh, core, y, zl], device(x, ys[k], z, core)) for k in (1, 3, 2)]
    width = GROUP * HEAD
    asked = []
    for layer in range(LAYERS):
        c = pltpu.make_async_copy(
            head_slice(q_ref, layer * KV_HEADS + y, width), qx_ref.at[y, layer], here_sem.at[2 + layer])
        c.start()
        local.append(c)
    for k in (1, 3, 2):
        for layer in range(LAYERS):
            asked.append(copies.send(
                head_slice(q_ref, layer * KV_HEADS + ys[k], width), qx_ref.at[y, layer], device(x, ys[k], z, core)))
    for k in (1, 3, 2):
        across[k].wait_recv()
        for h in (0, 1):
            ref = part(h, x, z, (y + 4 - k) % 4)
            for way in (0, 1):
                first[h, k, way] = copies.send(ref, ref, legs[h][way])
    for c in local[:3]:
        c.wait()

    def tell(places, to):
        for c in told:
            c.wait_recv()
        ref = notes_ref.at[places]
        return [copies.send(ref, ref, d) for d in to]

    told = tell((x, zh, core, every, zl), xs)

    given = []

    def share(half, bx, bz):
        ref = part(half, bx, bz, every)
        given.append(copies.send(ref, ref, beside))

    second = {}

    def onward(half, step, bx, bz):
        ref = part(half, bx, bz, every)
        for way in (0, 1):
            second[half, step, way] = copies.send(ref, ref, legs[1 - half][way])
        share(half, bx, bz)

    def came(half, way):
        if half == 0:
            return (nx[1 - way], z)
        return (x, nz[1 - way])

    for h in (0, 1):
        onward(h, 0, x, z)
    told = tell((every, zh, core, every, zl), zs)
    further = {}
    for k in (0, 1, 3, 2):
        way = 0 if k < 2 else 1
        for h in (0, 1):
            first[h, k, way].wait_recv()
            ref = part(h, *came(h, way), (y + 4 - k) % 4)
            further[h, k] = copies.send(ref, ref, legs[h][way])
    for way in (0, 1):
        for k in ((2, 3), (0, 1))[way]:
            for h in (0, 1):
                first[h, k, way].wait_recv()
        for h in (0, 1):
            onward(h, 1 + way, *came(h, way))
    told = tell((every, slice(None), core), [beside])
    for h in (0, 1):
        for k in range(4):
            further[h, k].wait_recv()
        opposite = ((x + 2) % 4, z) if h == 0 else (x, (z + 2) % 4)
        onward(h, 3, *opposite)

    def row_block(half, step):
        if half == 0:
            return [x, nx[1], nx[0], (x + 2) % 4][step]
        return [z, nz[1], nz[0], (z + 2) % 4][step]

    last = {}
    for step in range(4):
        for h in (0, 1):
            for way in (0, 1):
                second[h, step, way].wait_recv()
                b = row_block(h, step)
                bx, bz = (b, nz[1 - way]) if h == 0 else (nx[1 - way], b)
                ref = part(h, bx, bz, pl.ds(2 * way, 2))
                last[h, step, way] = copies.send(ref, ref, legs[1 - h][way])
                share(h, bx, bz)
    for step in range(4):
        for h in (0, 1):
            for way in (0, 1):
                last[h, step, way].wait_recv()
            b = row_block(h, step)
            share(h, *((b, (z + 2) % 4) if h == 0 else ((x + 2) % 4, b)))
    for c in given + told:
        c.wait_recv()
    for c in asked:
        c.wait_recv()
    for c in local[3:]:
        c.wait()
    copies.finish()


def gather(q, kv, document):
    anywhere = pl.BlockSpec(memory_space=pl.ANY)
    return pl.pallas_call(
        gather_kernel,
        out_shape=[
            jax.ShapeDtypeStruct((KV_HEADS, LAYERS, TOK, GROUP * HEAD), q.dtype),
            jax.ShapeDtypeStruct((2, 16, 4, 2, TOK, HEAD), kv.dtype),
            jax.ShapeDtypeStruct((4, 2, 2, 4, 2, 2, TOK), jnp.int32),
        ],
        in_specs=[anywhere] * 2 + [pl.BlockSpec(memory_space=pltpu.VMEM)],
        out_specs=[anywhere] * 3,
        scratch_shapes=[
            pltpu.VMEM((TOK, KV_HEADS * HEAD), kv.dtype),
            pltpu.VMEM((2, TOK), jnp.int32),
            pltpu.SemaphoreType.DMA((GATHER_COPIES,)),
            pltpu.SemaphoreType.DMA((GATHER_COPIES,)),
            pltpu.SemaphoreType.DMA((6,)),
        ],
        compiler_params=pltpu.CompilerParams(collective_id=0, has_side_effects=True),
    )(q, kv, document)


def return_kernel(o_ref, out_ref, send_sem, recv_sem, here_sem):
    x, y, z, core = place()
    ys = [(y + k) % 4 for k in range(4)]
    others = [device(x, ys[k], z, core) for k in (1, 3, 2)]
    greet(others)
    copies = Copies(send_sem, recv_sem)
    width = GROUP * HEAD

    def mine(layer):
        return out_ref.at[:, pl.ds(pl.multiple_of((layer * KV_HEADS + y) * width, width), width)]

    for k, to in zip((1, 3, 2), others):
        for layer in range(LAYERS):
            copies.send(o_ref.at[ys[k], layer], mine(layer), to)
    local = [pltpu.make_async_copy(o_ref.at[y, layer], mine(layer), here_sem.at[layer]) for layer in range(LAYERS)]
    for c in local:
        c.start()
    for c in local:
        c.wait()
    for c in copies.started:
        c.wait_recv()
    copies.finish()


def give_back(o):
    anywhere = pl.BlockSpec(memory_space=pl.ANY)
    return pl.pallas_call(
        return_kernel,
        out_shape=jax.ShapeDtypeStruct((TOK, LAYERS * Q_HEADS * HEAD), o.dtype),
        in_specs=[anywhere],
        out_specs=anywhere,
        scratch_shapes=[
            pltpu.SemaphoreType.DMA((6,)),
            pltpu.SemaphoreType.DMA((6,)),
            pltpu.SemaphoreType.DMA((2,)),
        ],
        compiler_params=pltpu.CompilerParams(collective_id=1, has_side_effects=True),
    )(o)


SCALE = 1.4426950408889634 * HEAD ** -0.5
NEG=-1e30
BIG = 100.0
KB = 512

def attend_kernel(kb, rg, chunk_ref, notes_ref, q_ref, kv_ref, o_ref, k_buf, v_buf, q_buf, o_buf, acc, top, sem, q_sem, o_sem):
    tiles = q_ref.shape[0]
    heads = LAYERS*GROUP
    rows = heads*TOK
    total = kv_ref.shape[1]
    piece = total//tiles
    sub = kb//TOK

    def kv_copies(i):
        src, dst = pl.ds(i*piece, piece), pl.ds(kb + i*piece, piece)
        return [pltpu.make_async_copy(kv_ref.at[0, src], k_buf.at[dst], sem.at[0, i]),
                pltpu.make_async_copy(kv_ref.at[1, src], v_buf.at[dst], sem.at[1, i])]

    def q_copies(t):
        return [pltpu.make_async_copy(q_ref.at[t, g//GROUP, :, pl.ds((g % GROUP)*HEAD, HEAD)],
                                      q_buf.at[t, pl.ds(g*TOK, TOK)], q_sem.at[t, g]) for g in range(heads)]

    def o_copies(t):
        return [pltpu.make_async_copy(o_buf.at[t, l], o_ref.at[t, l], o_sem.at[t, l]) for l in range(LAYERS)]

    for i in range(tiles):
        for c in q_copies(i) + kv_copies(i):
            c.start()
    k_buf[0:kb] = jnp.zeros((kb, HEAD), k_buf.dtype)
    v_buf[0:kb] = jnp.zeros((kb, HEAD), v_buf.dtype)
    ones = jnp.ones((kb, HEAD), v_buf.dtype)
    labels = notes_ref[:, 0, :]
    head = chunk_ref[tiles]
    lane = lax.broadcasted_iota(jnp.int32, (1, TOK), 1)
    longest = jnp.max(jnp.where(lane == head, jnp.max(notes_ref[:, 1, :], axis=0, keepdims=True), 0)).astype(jnp.float32)
    tri = lax.broadcasted_iota(jnp.int32, (TOK, TOK), 1) <= lax.broadcasted_iota(jnp.int32, (TOK, TOK), 0)

    for t in range(tiles):
        chunk = chunk_ref[t]
        end = (chunk + 1)*TOK
        mine = notes_ref[chunk, 0:1, :]
        low = jnp.min(mine, axis=1, keepdims=True)
        first = jnp.sum((labels < low).astype(jnp.int32))
        same = jnp.min(mine) == jnp.max(mine)
        span = end - first
        blocks = (span + kb - 1)//kb
        full = jnp.where(same, jnp.maximum(span//kb, 1), 1)
        qd = jnp.transpose(jnp.broadcast_to(mine, (TOK, TOK)))
        for c in q_copies(t) + kv_copies(t):
            c.wait()
        length = jnp.zeros((TOK, 1), jnp.float32)
        for g in range(heads):
            qf = q_buf[t, pl.ds(g*TOK, TOK), :].astype(jnp.float32)
            length = jnp.maximum(length, jnp.sum(qf*qf, axis=1, keepdims=True))
        small = jnp.max(length)*longest <= (BIG/SCALE)**2
        acc[...] = jnp.zeros_like(acc)

        def allowed(i):
            parts = []
            base = chunk + 1 - (i+1)*sub
            for s in range(sub):
                at = base + s
                m = (qd == notes_ref[jnp.maximum(at, 0), 0:1, :]) & (at >= 0)
                if s == sub-1:
                    m = m & (tri | (i > 0))
                parts.append(m)
            return jnp.concatenate(parts, axis=1)

        def quick(i, masked):
            at = pl.multiple_of(end - (i+1)*kb + kb, TOK)
            k = k_buf[pl.ds(at, kb), :]
            v = jnp.concatenate([v_buf[pl.ds(at, kb), :], ones], axis=1)
            if masked:
                mask = allowed(i)
            for g in range(rows//rg):
                r = pl.ds(g*rg, rg)
                s = lax.dot_general(q_buf[t, r, :], k, (((1,),(1,)),((),())), preferred_element_type=jnp.float32)
                p = jnp.exp2(s*SCALE)
                if masked:
                    p = jnp.where(jnp.concatenate([mask]*(rg//TOK), axis=0), p, 0.0)
                acc[r, :] += jnp.dot(p.astype(jnp.bfloat16), v, preferred_element_type=jnp.float32)

        def careful(i, masked):
            at = pl.multiple_of(end - (i+1)*kb + kb, TOK)
            k = k_buf[pl.ds(at, kb), :]
            v = jnp.concatenate([v_buf[pl.ds(at, kb), :], ones], axis=1)
            mask = allowed(i)
            for g in range(rows//TOK):
                r = pl.ds(g*TOK, TOK)
                s = lax.dot_general(q_buf[t, r, :], k, (((1,),(1,)),((),())), preferred_element_type=jnp.float32)*SCALE
                s = jnp.where(mask, s, NEG)
                old = top[r, :]
                new = jnp.maximum(old, jnp.max(s, axis=1, keepdims=True))
                top[r, :] = new
                p = jnp.where(mask, jnp.exp2(s - new[:, :1]), 0.0)
                keep = jnp.exp2(old - new)
                acc[r, :] = acc[r, :]*jnp.concatenate([keep, keep], axis=1) + jnp.dot(p.astype(jnp.bfloat16), v, preferred_element_type=jnp.float32)

        def at_masked(idx):
            return jnp.where(idx == 0, 0, idx - 1 + full)

        @pl.when(small)
        def _():
            lax.fori_loop(0, 1 + blocks - jnp.minimum(full, blocks), lambda n, _: quick(at_masked(n), True), None)
            lax.fori_loop(1, full, lambda n, _: quick(n, False), None)

        @pl.when(jnp.logical_not(small))
        def _():
            top[...] = jnp.full_like(top, NEG)
            lax.fori_loop(0, blocks, lambda n, _: careful(n, True), None)

        for l in range(LAYERS):
            for h in range(GROUP):
                r = pl.ds((l*GROUP+h)*TOK, TOK)
                a = acc[r, :]
                o_buf[t, l, :, h*HEAD:(h+1)*HEAD] = (a[:, :HEAD]/a[:, HEAD:]).astype(o_ref.dtype)
        for c in o_copies(t):
            c.start()
    for t in range(tiles):
        for c in o_copies(t):
            c.wait()


def attend(chunk, notes, q, kv, kb=KB, rg=256):
    tiles = q.shape[0]
    rows = LAYERS*GROUP*TOK
    total = kv.shape[1]
    anywhere = pl.BlockSpec(memory_space=pl.ANY)
    return pl.pallas_call(
        functools.partial(attend_kernel, kb, rg),
        out_shape=jax.ShapeDtypeStruct(q.shape, q.dtype),
        in_specs=[pl.BlockSpec(memory_space=pltpu.SMEM), pl.BlockSpec(memory_space=pltpu.VMEM), anywhere, anywhere],
        out_specs=anywhere,
        scratch_shapes=[
            pltpu.VMEM((kb + total, HEAD), jnp.bfloat16),
            pltpu.VMEM((kb + total, HEAD), jnp.bfloat16),
            pltpu.VMEM((tiles, rows, HEAD), jnp.bfloat16),
            pltpu.VMEM(q.shape, jnp.bfloat16),
            pltpu.VMEM((rows, 2*HEAD), jnp.float32),
            pltpu.VMEM((rows, HEAD), jnp.float32),
            pltpu.SemaphoreType.DMA((2, tiles)),
            pltpu.SemaphoreType.DMA((tiles, LAYERS*GROUP)),
            pltpu.SemaphoreType.DMA((tiles, LAYERS)),
        ],
        compiler_params=pltpu.CompilerParams(vmem_limit_bytes=50*2**20),
    )(chunk, notes, q, kv)


def shards(queries, shared_kv, document):
    row, col = lax.axis_index("qrow"), lax.axis_index("kvcol")
    qx, kvx, notes = gather(queries[0], shared_kv[:, 0], document[None])
    tiles = [t * 32 + (col % 2) * 16 + row for t in range(4)]
    chunk = jnp.stack(tiles + [col // 2]).astype(jnp.int32)
    o = attend(chunk, notes.reshape(-1, 2, TOK), qx, kvx.reshape(2, -1, HEAD))
    out = give_back(o)
    return out.reshape(queries.shape)


def solution(mesh):
    placed = (P("kvcol", "qrow", None), P(None, "qrow", "kvcol", None), P(("qrow", "kvcol")))
    return jax.shard_map(
        shards, mesh=mesh, in_specs=placed, out_specs=P("kvcol", "qrow", None), check_vma=False
    )
```

```python
import functools
import jax
import jax.numpy as jnp
from jax import lax
from jax.experimental import pallas as pl
from jax.experimental.pallas import tpu as pltpu
from jax.sharding import PartitionSpec as P

HEAD = 128
Q_HEADS = 16
KV_HEADS = 4
LAYERS = 2
GROUP = Q_HEADS // KV_HEADS
TOK = 128
MESH = pl.DeviceIdType.MESH


def place():
    row, col = lax.axis_index("qrow"), lax.axis_index("kvcol")
    return row // 4, col // 2, ((row // 2) % 2) * 2 + col % 2, row % 2


def row_of(x, z, core):
    return (x * 2 + z // 2) * 2 + core


def device(x, y, z, core):
    return (row_of(x, z, core), y * 2 + z % 2)


def greet(devices):
    barrier = pltpu.get_barrier_semaphore()
    for d in devices:
        pl.semaphore_signal(barrier, inc=1, device_id=d, device_id_type=MESH)
    pl.semaphore_wait(barrier, len(devices))


class Copies:
    def __init__(self, send_sem, recv_sem):
        self.send_sem, self.recv_sem, self.started = send_sem, recv_sem, []

    def send(self, src, dst, to):
        n = len(self.started)
        copy = pltpu.make_async_remote_copy(
            src_ref=src, dst_ref=dst, send_sem=self.send_sem.at[n], recv_sem=self.recv_sem.at[n],
            device_id=to, device_id_type=MESH,
        )
        copy.start()
        self.started.append(copy)
        return copy

    def finish(self):
        for copy in self.started:
            copy.wait_send()


GATHER_COPIES = 3 + 6 + 2 * (4 * 2 + 4 + 4 * 2 + 4 * 2) + 32 + 10


def gather_kernel(q_ref, kv_ref, doc_ref, qx_ref, kvx_ref, notes_ref, k_buf, note, send_sem, recv_sem, here_sem):
    x, y, z, core = place()
    col = lax.axis_index("kvcol")
    row = lax.axis_index("qrow")
    nx = [(x + 1) % 4, (x + 3) % 4]
    nz = [(z + 1) % 4, (z + 3) % 4]
    ys = [(y + k) % 4 for k in range(4)]
    beside = device(x, y, z, 1 - core)
    legs = {0: [device(v, y, z, core) for v in nx], 1: [device(x, y, v, core) for v in nz]}
    xs = [device((x + k) % 4, y, z, core) for k in (1, 3, 2)]
    zs = [device(x, y, (z + k) % 4, core) for k in (1, 3, 2)]
    greet(xs + zs + [beside] + [device(x, ys[k], z, core) for k in (1, 2, 3)])

    copies = Copies(send_sem, recv_sem)

    def part(half, bx, bz, which):
        return kvx_ref.at[half, row_of(bx, bz, core), which, bz % 2]

    def head_slice(ref, index, width):
        return ref.at[:, pl.ds(pl.multiple_of(index * width, width), width)]

    every = pl.ds(0, 4)
    own = [head_slice(kv_ref.at[h], y, HEAD) for h in (0, 1)]
    local = []
    for h in (0, 1):
        c = pltpu.make_async_copy(own[h], part(h, x, z, y), here_sem.at[h])
        c.start()
        local.append(c)
    first = {}
    for h in (0, 1):
        for way in (0, 1):
            first[h, 0, way] = copies.send(own[h], part(h, x, z, y), legs[h][way])
    across = {}
    for k in (1, 3, 2):
        src = kv_ref.at[:, :, pl.ds(pl.multiple_of(ys[k] * HEAD, HEAD), HEAD)]
        across[k] = copies.send(src, kvx_ref.at[:, row, y, z % 2], device(x, ys[k], z, core))
    c = pltpu.make_async_copy(kv_ref.at[0], k_buf, here_sem.at[4])
    c.start()
    c.wait()
    lane = lax.broadcasted_iota(jnp.int32, (1, TOK), 1)
    lengths = jnp.zeros((1, TOK), jnp.int32)
    for h in range(KV_HEADS):
        k = k_buf[:, h * HEAD:(h + 1) * HEAD].astype(jnp.float32)
        most = jnp.max(jnp.sum(k * k, axis=1, keepdims=True), axis=0, keepdims=True)
        lengths = jnp.where(lane == h, most.astype(jnp.int32) + 1, lengths)
    note[0:1, :] = doc_ref[...]
    note[1:2, :] = lengths
    zh, zl = z // 2, z % 2
    c = pltpu.make_async_copy(note, notes_ref.at[x, zh, core, y, zl], here_sem.at[5])
    c.start()
    local.append(c)
    told = [copies.send(note, notes_ref.at[x, zh, core, y, zl], device(x, ys[k], z, core)) for k in (1, 3, 2)]
    width = GROUP * HEAD
    asked = []
    for layer in range(LAYERS):
        c = pltpu.make_async_copy(
            head_slice(q_ref, layer * KV_HEADS + y, width), qx_ref.at[y, layer], here_sem.at[2 + layer])
        c.start()
        local.append(c)
    for k in (1, 3, 2):
        for layer in range(LAYERS):
            asked.append(copies.send(
                head_slice(q_ref, layer * KV_HEADS + ys[k], width), qx_ref.at[y, layer], device(x, ys[k], z, core)))
    for k in (1, 3, 2):
        across[k].wait_recv()
        for h in (0, 1):
            ref = part(h, x, z, (y + 4 - k) % 4)
            for way in (0, 1):
                first[h, k, way] = copies.send(ref, ref, legs[h][way])
    for c in local[:3]:
        c.wait()

    def tell(places, to):
        for c in told:
            c.wait_recv()
        ref = notes_ref.at[places]
        return [copies.send(ref, ref, d) for d in to]

    told = tell((x, zh, core, every, zl), xs)

    given = []

    def share(half, bx, bz):
        ref = part(half, bx, bz, every)
        given.append(copies.send(ref, ref, beside))

    second = {}

    def onward(half, step, bx, bz):
        ref = part(half, bx, bz, every)
        for way in (0, 1):
            second[half, step, way] = copies.send(ref, ref, legs[1 - half][way])
        share(half, bx, bz)

    def came(half, way):
        if half == 0:
            return (nx[1 - way], z)
        return (x, nz[1 - way])

    for h in (0, 1):
        onward(h, 0, x, z)
    told = tell((every, zh, core, every, zl), zs)
    further = {}
    for k in (0, 1, 3, 2):
        way = 0 if k < 2 else 1
        for h in (0, 1):
            first[h, k, way].wait_recv()
            ref = part(h, *came(h, way), (y + 4 - k) % 4)
            further[h, k] = copies.send(ref, ref, legs[h][way])
    for way in (0, 1):
        for k in ((2, 3), (0, 1))[way]:
            for h in (0, 1):
                first[h, k, way].wait_recv()
        for h in (0, 1):
            onward(h, 1 + way, *came(h, way))
    told = tell((every, slice(None), core), [beside])
    for h in (0, 1):
        for k in range(4):
            further[h, k].wait_recv()
        opposite = ((x + 2) % 4, z) if h == 0 else (x, (z + 2) % 4)
        onward(h, 3, *opposite)

    def row_block(half, step):
        if half == 0:
            return [x, nx[1], nx[0], (x + 2) % 4][step]
        return [z, nz[1], nz[0], (z + 2) % 4][step]

    last = {}
    for step in range(4):
        for h in (0, 1):
            for way in (0, 1):
                second[h, step, way].wait_recv()
                b = row_block(h, step)
                bx, bz = (b, nz[1 - way]) if h == 0 else (nx[1 - way], b)
                ref = part(h, bx, bz, pl.ds(2 * way, 2))
                last[h, step, way] = copies.send(ref, ref, legs[1 - h][way])
                share(h, bx, bz)
    for step in range(4):
        for h in (0, 1):
            for way in (0, 1):
                last[h, step, way].wait_recv()
            b = row_block(h, step)
            share(h, *((b, (z + 2) % 4) if h == 0 else ((x + 2) % 4, b)))
    for c in given + told:
        c.wait_recv()
    for c in asked:
        c.wait_recv()
    for c in local[3:]:
        c.wait()
    copies.finish()


def gather(q, kv, document):
    anywhere = pl.BlockSpec(memory_space=pltpu.HBM)
    return pl.pallas_call(
        gather_kernel,
        out_shape=[
            jax.ShapeDtypeStruct((KV_HEADS, LAYERS, TOK, GROUP * HEAD), q.dtype),
            jax.ShapeDtypeStruct((2, 16, 4, 2, TOK, HEAD), kv.dtype),
            jax.ShapeDtypeStruct((4, 2, 2, 4, 2, 2, TOK), jnp.int32),
        ],
        in_specs=[anywhere] * 2 + [pl.BlockSpec(memory_space=pltpu.VMEM)],
        out_specs=[anywhere, pl.BlockSpec(memory_space=pltpu.VMEM), pl.BlockSpec(memory_space=pltpu.VMEM)],
        scratch_shapes=[
            pltpu.VMEM((TOK, KV_HEADS * HEAD), kv.dtype),
            pltpu.VMEM((2, TOK), jnp.int32),
            pltpu.SemaphoreType.DMA((GATHER_COPIES,)),
            pltpu.SemaphoreType.DMA((GATHER_COPIES,)),
            pltpu.SemaphoreType.DMA((6,)),
        ],
        compiler_params=pltpu.CompilerParams(collective_id=0, has_side_effects=True, vmem_limit_bytes=16 * 2**20),
    )(q, kv, document)


def return_kernel(o_ref, out_ref, send_sem, recv_sem, here_sem):
    x, y, z, core = place()
    ys = [(y + k) % 4 for k in range(4)]
    others = [device(x, ys[k], z, core) for k in (1, 3, 2)]
    greet(others)
    copies = Copies(send_sem, recv_sem)
    width = GROUP * HEAD

    def mine(layer):
        return out_ref.at[:, pl.ds(pl.multiple_of((layer * KV_HEADS + y) * width, width), width)]

    for k, to in zip((1, 3, 2), others):
        for layer in range(LAYERS):
            copies.send(o_ref.at[ys[k], layer], mine(layer), to)
    local = [pltpu.make_async_copy(o_ref.at[y, layer], mine(layer), here_sem.at[layer]) for layer in range(LAYERS)]
    for c in local:
        c.start()
    for c in local:
        c.wait()
    for c in copies.started:
        c.wait_recv()
    copies.finish()


def give_back(o):
    anywhere = pl.BlockSpec(memory_space=pltpu.HBM)
    return pl.pallas_call(
        return_kernel,
        out_shape=jax.ShapeDtypeStruct((TOK, LAYERS * Q_HEADS * HEAD), o.dtype),
        in_specs=[anywhere],
        out_specs=pl.BlockSpec(memory_space=pltpu.VMEM),
        scratch_shapes=[
            pltpu.SemaphoreType.DMA((6,)),
            pltpu.SemaphoreType.DMA((6,)),
            pltpu.SemaphoreType.DMA((2,)),
        ],
        compiler_params=pltpu.CompilerParams(collective_id=1, has_side_effects=True, vmem_limit_bytes=16 * 2**20),
    )(o)


SCALE = 1.4426950408889634 * HEAD ** -0.5
NEG=-1e30
BIG = 100.0
KB = 512
KI = 1024

def attend_kernel(kb, ki, chunk_ref, notes_ref, q_ref, kv_ref, o_ref, q_buf, o_buf, acc, top, q_sem, o_sem):
    tiles = q_ref.shape[0]
    heads = LAYERS*GROUP
    rows = heads*TOK
    sub = kb//TOK

    def q_copies(t):
        return [pltpu.make_async_copy(q_ref.at[t, g//GROUP, :, pl.ds((g % GROUP)*HEAD, HEAD)],
                                      q_buf.at[t, pl.ds(g*TOK, TOK)], q_sem.at[t, g]) for g in range(heads)]

    def o_copies(t):
        return [pltpu.make_async_copy(o_buf.at[t, l], o_ref.at[t, l], o_sem.at[t, l]) for l in range(LAYERS)]

    for i in range(tiles):
        for c in q_copies(i):
            c.start()
    labels = notes_ref[:, 0, :]
    head = chunk_ref[tiles]
    lane = lax.broadcasted_iota(jnp.int32, (1, TOK), 1)
    longest = jnp.max(jnp.where(lane == head, jnp.max(notes_ref[:, 1, :], axis=0, keepdims=True), 0)).astype(jnp.float32)
    tri = lax.broadcasted_iota(jnp.int32, (TOK, TOK), 0) <= lax.broadcasted_iota(jnp.int32, (TOK, TOK), 1)

    bounds = []
    for t in range(tiles):
        chunk = chunk_ref[t]
        mine = notes_ref[chunk, 0:1, :]
        low = jnp.min(mine, axis=1, keepdims=True)
        bounds.append((chunk, jnp.sum((labels < low).astype(jnp.int32)), jnp.min(mine) == jnp.max(mine)))
    length = jnp.zeros((TOK, 1), jnp.float32)
    for t in range(tiles):
        for c in q_copies(t):
            c.wait()
        for g in range(heads):
            qf = q_buf[t, pl.ds(g*TOK, TOK), :].astype(jnp.float32)
            length = jnp.maximum(length, jnp.sum(qf*qf, axis=1, keepdims=True))
    small = jnp.max(length)*longest <= (BIG/SCALE)**2

    for t in range(tiles):
        chunk, first, same = bounds[t]
        end = (chunk + 1)*TOK
        mine = notes_ref[chunk, 0:1, :]
        span = jnp.maximum(end - first - kb, 0)
        full = jnp.where(same, span//ki, 0)
        edges = 1 + (span - full*ki + kb - 1)//kb
        acc[...] = jnp.zeros_like(acc)

        def edge(n):
            back = jnp.where(n == 0, 0, n*kb + full*ki)
            parts = []
            stop = chunk + 1 - back//TOK
            start = jnp.maximum(stop - sub, 0)
            for s in range(sub):
                at = start + s
                label = jnp.transpose(jnp.broadcast_to(notes_ref[at, 0:1, :], (TOK, TOK)))
                parts.append((label == mine) & (at < stop) & (tri | (at != chunk)))
            return start*TOK, jnp.concatenate(parts, axis=0)

        def block(start, size):
            at = pl.ds(pl.multiple_of(start, TOK), size)
            v = jnp.concatenate([jnp.transpose(kv_ref[1, at, :]), jnp.ones((16, size), kv_ref.dtype)], axis=0)
            return kv_ref[0, at, :], v

        def inner(n):
            return end - kb - (n + 1)*ki

        def dot_q(k, r):
            return lax.dot_general(k, q_buf[t, r, :], (((1,), (1,)), ((), ())), preferred_element_type=jnp.float32)*SCALE

        def quick(n, _):
            k, v = block(inner(n), ki)
            p = jnp.exp2(dot_q(k, pl.ds(0, rows)))
            acc[...] += jnp.dot(v, p.astype(v.dtype), preferred_element_type=jnp.float32)

        def quick_edge(n, _):
            start, mask = edge(n)
            k, v = block(start, kb)
            p = jnp.exp2(dot_q(k, pl.ds(0, rows)))
            p = jnp.where(jnp.concatenate([mask]*heads, axis=1), p, 0.0)
            acc[...] += jnp.dot(v, p.astype(v.dtype), preferred_element_type=jnp.float32)

        def careful(k, v, mask):
            for g in range(heads):
                r = pl.ds(g*TOK, TOK)
                s = dot_q(k, r)
                if mask is not None:
                    s = jnp.where(mask, s, NEG)
                old = top[0:1, r]
                new = jnp.maximum(old, jnp.max(s, axis=0, keepdims=True))
                top[0:1, r] = new
                p = jnp.exp2(s - new)
                if mask is not None:
                    p = jnp.where(mask, p, 0.0)
                acc[:, r] = acc[:, r]*jnp.exp2(old - new) + jnp.dot(v, p.astype(v.dtype), preferred_element_type=jnp.float32)

        def careful_full(n, _):
            careful(*block(inner(n), ki), None)

        def careful_edge(n, _):
            start, mask = edge(n)
            careful(*block(start, kb), mask)

        @pl.when(small)
        def _():
            lax.fori_loop(0, edges, quick_edge, None)
            lax.fori_loop(0, full, quick, None)

        @pl.when(jnp.logical_not(small))
        def _():
            top[...] = jnp.full_like(top, NEG)
            lax.fori_loop(0, edges, careful_edge, None)
            lax.fori_loop(0, full, careful_full, None)

        for g in range(heads):
            r = pl.ds(g*TOK, TOK)
            o = acc[:HEAD, r]/acc[HEAD:HEAD + 1, r]
            h = g % GROUP
            o_buf[t, g//GROUP, :, h*HEAD:(h + 1)*HEAD] = jnp.transpose(o).astype(o_buf.dtype)
        for c in o_copies(t):
            c.start()
    for t in range(tiles):
        for c in o_copies(t):
            c.wait()


def attend(chunk, notes, q, kv, kb=KB, ki=KI):
    tiles = q.shape[0]
    rows = LAYERS*GROUP*TOK
    anywhere = pl.BlockSpec(memory_space=pltpu.HBM)
    return pl.pallas_call(
        functools.partial(attend_kernel, kb, ki),
        out_shape=jax.ShapeDtypeStruct(q.shape, q.dtype),
        in_specs=[pl.BlockSpec(memory_space=pltpu.SMEM), pl.BlockSpec(memory_space=pltpu.VMEM), anywhere, pl.BlockSpec(memory_space=pltpu.VMEM)],
        out_specs=anywhere,
        scratch_shapes=[
            pltpu.VMEM((tiles, rows, HEAD), jnp.bfloat16),
            pltpu.VMEM(q.shape, jnp.bfloat16),
            pltpu.VMEM((HEAD + 16, rows), jnp.float32),
            pltpu.VMEM((8, rows), jnp.float32),
            pltpu.SemaphoreType.DMA((tiles, LAYERS*GROUP)),
            pltpu.SemaphoreType.DMA((tiles, LAYERS)),
        ],
        compiler_params=pltpu.CompilerParams(vmem_limit_bytes=40*2**20),
    )(chunk, notes, q, kv)


def shards(queries, shared_kv, document):
    row, col = lax.axis_index("qrow"), lax.axis_index("kvcol")
    qx, kvx, notes = gather(queries[0], shared_kv[:, 0], document[None])
    tiles = [t * 32 + (col % 2) * 16 + row for t in range(4)]
    chunk = jnp.stack(tiles + [col // 2]).astype(jnp.int32)
    o = attend(chunk, notes.reshape(-1, 2, TOK), qx, kvx.reshape(2, -1, HEAD))
    out = give_back(o)
    return out.reshape(queries.shape)


def solution(mesh):
    placed = (P("kvcol", "qrow", None), P(None, "qrow", "kvcol", None), P(("qrow", "kvcol")))
    return jax.shard_map(
        shards, mesh=mesh, in_specs=placed, out_specs=P("kvcol", "qrow", None), check_vma=False
    )
```

```python
import functools
import jax
import jax.numpy as jnp
from jax import lax
from jax.experimental import pallas as pl
from jax.experimental.pallas import tpu as pltpu
from jax.sharding import PartitionSpec as P

HEAD = 128
Q_HEADS = 16
KV_HEADS = 4
LAYERS = 2
GROUP = Q_HEADS // KV_HEADS
TOK = 128
MESH = pl.DeviceIdType.MESH


def place():
    row, col = lax.axis_index("qrow"), lax.axis_index("kvcol")
    return row // 4, col // 2, ((row // 2) % 2) * 2 + col % 2, row % 2


def row_of(x, z, core):
    return (x * 2 + z // 2) * 2 + core


def device(x, y, z, core):
    return (row_of(x, z, core), y * 2 + z % 2)


def greet(devices):
    barrier = pltpu.get_barrier_semaphore()
    for d in devices:
        pl.semaphore_signal(barrier, inc=1, device_id=d, device_id_type=MESH)
    pl.semaphore_wait(barrier, len(devices))


class Copies:
    def __init__(self, send_sem, recv_sem):
        self.send_sem, self.recv_sem, self.started = send_sem, recv_sem, []

    def send(self, src, dst, to):
        n = len(self.started)
        copy = pltpu.make_async_remote_copy(
            src_ref=src, dst_ref=dst, send_sem=self.send_sem.at[n], recv_sem=self.recv_sem.at[n],
            device_id=to, device_id_type=MESH,
        )
        copy.start()
        self.started.append(copy)
        return copy

    def finish(self):
        for copy in self.started:
            copy.wait_send()


GATHER_COPIES = 3 + 6 + 2 * (4 * 2 + 4 + 7 * 2 + 4 * 2) + 32 + 10


def gather_kernel(q_ref, kv_ref, doc_ref, heads_ref, length_ref, kvx_ref, notes_ref, qx_ref, note, send_sem, recv_sem):
    x, y, z, core = place()
    col = lax.axis_index("kvcol")
    row = lax.axis_index("qrow")
    nx = [(x + 1) % 4, (x + 3) % 4]
    nz = [(z + 1) % 4, (z + 3) % 4]
    ys = [(y + k) % 4 for k in range(4)]
    beside = device(x, y, z, 1 - core)
    legs = {0: [device(v, y, z, core) for v in nx], 1: [device(x, y, v, core) for v in nz]}
    xs = [device((x + k) % 4, y, z, core) for k in (1, 3, 2)]
    zs = [device(x, y, (z + k) % 4, core) for k in (1, 3, 2)]
    greet(xs + zs + [beside] + [device(x, ys[k], z, core) for k in (1, 2, 3)])

    copies = Copies(send_sem, recv_sem)

    def part(half, bx, bz, which):
        return kvx_ref.at[half, row_of(bx, bz, core), which, bz % 2]

    def head_slice(ref, index, width):
        return ref.at[:, pl.ds(pl.multiple_of(index * width, width), width)]

    every = pl.ds(0, 4)
    own = [head_slice(kv_ref.at[h], y, HEAD) for h in (0, 1)]
    first = {}
    for h in (0, 1):
        for way in (0, 1):
            first[h, 0, way] = copies.send(own[h], part(h, x, z, y), legs[h][way])
    second = {}
    for h in (0, 1):
        for way in (0, 1):
            second[h, 0, way] = [copies.send(own[h], part(h, x, z, y), legs[1 - h][way])]
    across = {}
    for k in (1, 3, 2):
        src = kv_ref.at[:, :, pl.ds(pl.multiple_of(ys[k] * HEAD, HEAD), HEAD)]
        across[k] = copies.send(src, kvx_ref.at[:, row, y, z % 2], device(x, ys[k], z, core))
    for v in range(KV_HEADS):
        @pl.when(y == v)
        def _():
            for h in (0, 1):
                kvx_ref[h, row, v, z % 2] = kv_ref[h, :, v * HEAD:(v + 1) * HEAD]
            for layer in range(LAYERS):
                at = (layer * KV_HEADS + v) * GROUP * HEAD
                qx_ref[v, layer] = q_ref[:, at:at + GROUP * HEAD]

    lane = lax.broadcasted_iota(jnp.int32, (1, TOK), 1)
    lengths = jnp.zeros((1, TOK), jnp.int32)
    for h in range(KV_HEADS):
        k = kv_ref[0, :, h * HEAD:(h + 1) * HEAD].astype(jnp.float32)
        most = jnp.max(jnp.sum(k * k, axis=1, keepdims=True), axis=0, keepdims=True)
        lengths = jnp.where(lane == h, most.astype(jnp.int32) + 1, lengths)
    note[0:1, :] = doc_ref[...]
    note[1:2, :] = lengths
    zh, zl = z // 2, z % 2
    notes_ref[x, zh, core, y, zl] = note[...]
    told = [copies.send(note, notes_ref.at[x, zh, core, y, zl], device(x, ys[k], z, core)) for k in (1, 3, 2)]
    for k in (1, 3, 2):
        across[k].wait_recv()
        for h in (0, 1):
            ref = part(h, x, z, (y + 4 - k) % 4)
            for way in (0, 1):
                first[h, k, way] = copies.send(ref, ref, legs[h][way])
        for h in (0, 1):
            ref = part(h, x, z, (y + 4 - k) % 4)
            for way in (0, 1):
                second[h, 0, way].append(copies.send(ref, ref, legs[1 - h][way]))

    width = GROUP * HEAD
    asked = []
    for k in (1, 3, 2):
        for layer in range(LAYERS):
            asked.append(copies.send(
                head_slice(q_ref, layer * KV_HEADS + ys[k], width), qx_ref.at[y, layer], device(x, ys[k], z, core)))
    def tell(places, to):
        for c in told:
            c.wait_recv()
        ref = notes_ref.at[places]
        return [copies.send(ref, ref, d) for d in to]

    told = tell((x, zh, core, every, zl), xs)

    given = []

    def share(half, bx, bz):
        ref = part(half, bx, bz, every)
        given.append(copies.send(ref, ref, beside))

    def onward(half, step, bx, bz):
        ref = part(half, bx, bz, every)
        for way in (0, 1):
            second[half, step, way] = [copies.send(ref, ref, legs[1 - half][way])]
        share(half, bx, bz)

    def came(half, way):
        if half == 0:
            return (nx[1 - way], z)
        return (x, nz[1 - way])

    for h in (0, 1):
        share(h, x, z)
    further = {}
    for k in (0, 1, 3, 2):
        way = 0 if k < 2 else 1
        for h in (0, 1):
            first[h, k, way].wait_recv()
            ref = part(h, *came(h, way), (y + 4 - k) % 4)
            further[h, k] = copies.send(ref, ref, legs[h][way])
    for way in (0, 1):
        for k in ((2, 3), (0, 1))[way]:
            for h in (0, 1):
                first[h, k, way].wait_recv()
        for h in (0, 1):
            onward(h, 1 + way, *came(h, way))
    told = tell((every, zh, core, every, zl), zs)
    for h in (0, 1):
        for k in range(4):
            further[h, k].wait_recv()
        opposite = ((x + 2) % 4, z) if h == 0 else (x, (z + 2) % 4)
        onward(h, 3, *opposite)

    def row_block(half, step):
        if half == 0:
            return [x, nx[1], nx[0], (x + 2) % 4][step]
        return [z, nz[1], nz[0], (z + 2) % 4][step]

    last = {}
    for step in range(4):
        if step == 2:
            told = tell((every, slice(None), core), [beside])
        for h in (0, 1):
            for way in (0, 1):
                for c in second[h, step, way]:
                    c.wait_recv()
                b = row_block(h, step)
                bx, bz = (b, nz[1 - way]) if h == 0 else (nx[1 - way], b)
                ref = part(h, bx, bz, pl.ds(2 * way, 2))
                last[h, step, way] = copies.send(ref, ref, legs[1 - h][way])
                share(h, bx, bz)
    for c in asked:
        c.wait_recv()
    length = jnp.zeros((TOK, 1), jnp.float32)
    for t in range(4):
        for g in range(LAYERS * GROUP):
            head = qx_ref[t, g // GROUP, :, (g % GROUP) * HEAD:(g % GROUP + 1) * HEAD]
            heads_ref[t, g * TOK:(g + 1) * TOK, :] = head
            head = head.astype(jnp.float32)
            length = jnp.maximum(length, jnp.sum(head * head, axis=1, keepdims=True))
    length_ref[...] = jnp.broadcast_to(jnp.max(length, axis=0, keepdims=True), (1, TOK))
    for step in range(4):
        for h in (0, 1):
            for way in (0, 1):
                last[h, step, way].wait_recv()
            b = row_block(h, step)
            share(h, *((b, (z + 2) % 4) if h == 0 else ((x + 2) % 4, b)))
    for c in given + told:
        c.wait_recv()
    copies.finish()


def gather(q, kv, document):
    return pl.pallas_call(
        gather_kernel,
        out_shape=[
            jax.ShapeDtypeStruct((KV_HEADS, LAYERS * GROUP * TOK, HEAD), q.dtype),
            jax.ShapeDtypeStruct((1, TOK), jnp.float32),
            jax.ShapeDtypeStruct((2, 16, 4, 2, TOK, HEAD), kv.dtype),
            jax.ShapeDtypeStruct((4, 2, 2, 4, 2, 2, TOK), jnp.int32),
        ],
        in_specs=[pl.BlockSpec(memory_space=pltpu.VMEM)] * 3,
        out_specs=[pl.BlockSpec(memory_space=pltpu.VMEM)] * 4,
        scratch_shapes=[
            pltpu.VMEM((KV_HEADS, LAYERS, TOK, GROUP * HEAD), q.dtype),
            pltpu.VMEM((2, TOK), jnp.int32),
            pltpu.SemaphoreType.DMA((GATHER_COPIES,)),
            pltpu.SemaphoreType.DMA((GATHER_COPIES,)),
        ],
        compiler_params=pltpu.CompilerParams(collective_id=0, has_side_effects=True, vmem_limit_bytes=16 * 2**20),
    )(q, kv, document)


def return_kernel(o_ref, out_ref, send_sem, recv_sem):
    x, y, z, core = place()
    ys = [(y + k) % 4 for k in range(4)]
    others = [device(x, ys[k], z, core) for k in (1, 3, 2)]
    greet(others)
    copies = Copies(send_sem, recv_sem)
    width = GROUP * HEAD

    def mine(layer):
        return out_ref.at[:, pl.ds(pl.multiple_of((layer * KV_HEADS + y) * width, width), width)]

    for k, to in zip((1, 3, 2), others):
        for layer in range(LAYERS):
            copies.send(o_ref.at[ys[k], layer], mine(layer), to)
    for v in range(KV_HEADS):
        @pl.when(y == v)
        def _():
            for layer in range(LAYERS):
                at = (layer * KV_HEADS + v) * width
                out_ref[:, at:at + width] = o_ref[v, layer]
    for c in copies.started:
        c.wait_recv()
    copies.finish()


def give_back(o):
    return pl.pallas_call(
        return_kernel,
        out_shape=jax.ShapeDtypeStruct((TOK, LAYERS * Q_HEADS * HEAD), o.dtype),
        in_specs=[pl.BlockSpec(memory_space=pltpu.VMEM)],
        out_specs=pl.BlockSpec(memory_space=pltpu.VMEM),
        scratch_shapes=[
            pltpu.SemaphoreType.DMA((6,)),
            pltpu.SemaphoreType.DMA((6,)),
        ],
        compiler_params=pltpu.CompilerParams(collective_id=1, has_side_effects=True, vmem_limit_bytes=16 * 2**20),
    )(o)


SCALE = 1.4426950408889634 * HEAD ** -0.5
NEG=-1e30
BIG = 100.0
KB = 512
KI = 1024

def attend_kernel(kb, ki, chunk_ref, notes_ref, length_ref, q_ref, kv_ref, o_ref, acc, top):
    tiles = q_ref.shape[0]
    heads = LAYERS*GROUP
    rows = heads*TOK

    labels = notes_ref[:, 0, :]
    head = chunk_ref[tiles]
    lane = lax.broadcasted_iota(jnp.int32, (1, TOK), 1)
    longest = jnp.max(jnp.where(lane == head, jnp.max(notes_ref[:, 1, :], axis=0, keepdims=True), 0)).astype(jnp.float32)
    bounds = []
    for t in range(tiles):
        chunk = chunk_ref[t]
        mine = notes_ref[chunk, 0:1, :]
        low = jnp.min(mine, axis=1, keepdims=True)
        bounds.append((chunk, jnp.sum((labels < low).astype(jnp.int32))))
    small = jnp.max(length_ref[...])*longest <= (BIG/SCALE)**2

    for t in range(tiles):
        chunk, first = bounds[t]
        end = (chunk + 1)*TOK
        mine = notes_ref[chunk, 0:1, :]
        span = jnp.maximum(end - first - kb, 0)
        full = span//ki
        edges = 1 + (span - full*ki + kb - 1)//kb
        acc[...] = jnp.zeros_like(acc)
        below = jnp.transpose(jnp.broadcast_to(mine, (TOK, TOK))) < mine
        inside = end - TOK + jnp.sum(below.astype(jnp.int32), axis=0, keepdims=True)
        ahead = mine == jnp.min(mine, axis=1, keepdims=True)
        lowest = jnp.where(ahead, first, inside)
        ahead = jnp.concatenate([ahead]*heads, axis=1)
        place = end - TOK + lax.broadcasted_iota(jnp.int32, (1, TOK), 1)

        def edge(n):
            stop = end - jnp.where(n == 0, 0, n*kb + full*ki)
            start = jnp.maximum(stop - kb, 0)
            key = start + lax.broadcasted_iota(jnp.int32, (kb, TOK), 0)
            return start, (key >= lowest) & (key <= jnp.minimum(place, stop - 1))

        def block(start, size):
            at = pl.ds(pl.multiple_of(start, TOK), size)
            v = jnp.concatenate([jnp.transpose(kv_ref[1, at, :]), jnp.ones((16, size), kv_ref.dtype)], axis=0)
            return kv_ref[0, at, :], v

        def inner(n):
            return end - kb - (n + 1)*ki

        def dot_q(k, r):
            return lax.dot_general(k, q_ref[t, r, :], (((1,), (1,)), ((), ())), preferred_element_type=jnp.float32)*SCALE

        def quick(n, _):
            k, v = block(inner(n), ki)
            p = jnp.exp2(dot_q(k, pl.ds(0, rows)))
            acc[...] += jnp.dot(v, p.astype(v.dtype), preferred_element_type=jnp.float32)

        def quick_edge(n, _):
            start, mask = edge(n)
            k, v = block(start, kb)
            p = jnp.exp2(dot_q(k, pl.ds(0, rows)))
            p = jnp.where(jnp.concatenate([mask]*heads, axis=1), p, 0.0)
            acc[...] += jnp.dot(v, p.astype(v.dtype), preferred_element_type=jnp.float32)

        def careful(k, v, mask):
            for g in range(heads):
                r = pl.ds(g*TOK, TOK)
                s = dot_q(k, r)
                if mask is not None:
                    s = jnp.where(mask, s, NEG)
                old = top[0:1, r]
                new = jnp.maximum(old, jnp.max(s, axis=0, keepdims=True))
                top[0:1, r] = new
                p = jnp.exp2(s - new)
                if mask is not None:
                    p = jnp.where(mask, p, 0.0)
                acc[:, r] = acc[:, r]*jnp.exp2(old - new) + jnp.dot(v, p.astype(v.dtype), preferred_element_type=jnp.float32)

        def careful_full(n, _):
            careful(*block(inner(n), ki), None)

        def careful_edge(n, _):
            start, mask = edge(n)
            careful(*block(start, kb), mask)

        @pl.when(small)
        def _():
            lax.fori_loop(0, full, quick, None)
            acc[...] = jnp.where(ahead, acc[...], 0.0)
            lax.fori_loop(0, edges, quick_edge, None)

        @pl.when(jnp.logical_not(small))
        def _():
            top[...] = jnp.full_like(top, NEG)
            lax.fori_loop(0, full, careful_full, None)
            acc[...] = jnp.where(ahead, acc[...], 0.0)
            top[...] = jnp.where(ahead, top[...], NEG)
            lax.fori_loop(0, edges, careful_edge, None)

        for g in range(heads):
            r = pl.ds(g*TOK, TOK)
            o = acc[:HEAD, r]/acc[HEAD:HEAD + 1, r]
            h = g % GROUP
            o_ref[t, g//GROUP, :, h*HEAD:(h + 1)*HEAD] = jnp.transpose(o).astype(o_ref.dtype)


def attend(chunk, notes, length, q, kv, kb=KB, ki=KI):
    tiles, rows, _ = q.shape
    shape = (tiles, LAYERS, TOK, GROUP*HEAD)
    vmem = pl.BlockSpec(memory_space=pltpu.VMEM)
    return pl.pallas_call(
        functools.partial(attend_kernel, kb, ki),
        out_shape=jax.ShapeDtypeStruct(shape, q.dtype),
        in_specs=[pl.BlockSpec(memory_space=pltpu.SMEM)] + [vmem]*4,
        out_specs=vmem,
        scratch_shapes=[
            pltpu.VMEM((HEAD + 16, rows), jnp.float32),
            pltpu.VMEM((8, rows), jnp.float32),
        ],
        compiler_params=pltpu.CompilerParams(vmem_limit_bytes=40*2**20),
    )(chunk, notes, length, q, kv)


def shards(queries, shared_kv, document):
    row, col = lax.axis_index("qrow"), lax.axis_index("kvcol")
    heads, length, kvx, notes = gather(queries[0], shared_kv[:, 0], document[None])
    tiles = [t * 32 + (col % 2) * 16 + row for t in range(4)]
    chunk = jnp.stack(tiles + [col // 2]).astype(jnp.int32)
    o = attend(chunk, notes.reshape(-1, 2, TOK), length, heads, kvx.reshape(2, -1, HEAD))
    out = give_back(o)
    return out.reshape(queries.shape)


def solution(mesh):
    placed = (P("kvcol", "qrow", None), P(None, "qrow", "kvcol", None), P(("qrow", "kvcol")))
    return jax.shard_map(
        shards, mesh=mesh, in_specs=placed, out_specs=P("kvcol", "qrow", None), check_vma=False
    )
```

```python
import functools
import jax
import jax.numpy as jnp
from jax import lax
from jax.experimental import pallas as pl
from jax.experimental.pallas import tpu as pltpu
from jax.sharding import PartitionSpec as P

HEAD = 128
Q_HEADS = 16
KV_HEADS = 4
LAYERS = 2
GROUP = Q_HEADS // KV_HEADS
TOK = 128
MESH = pl.DeviceIdType.MESH


def place():
    row, col = lax.axis_index("qrow"), lax.axis_index("kvcol")
    return row // 4, col // 2, ((row // 2) % 2) * 2 + col % 2, row % 2


def row_of(x, z, core):
    return (x * 2 + z // 2) * 2 + core


def device(x, y, z, core):
    return (row_of(x, z, core), y * 2 + z % 2)


def greet(devices):
    barrier = pltpu.get_barrier_semaphore()
    for d in devices:
        pl.semaphore_signal(barrier, inc=1, device_id=d, device_id_type=MESH)
    pl.semaphore_wait(barrier, len(devices))


class Copies:
    def __init__(self, send_sem, recv_sem):
        self.send_sem, self.recv_sem, self.started = send_sem, recv_sem, []

    def send(self, src, dst, to):
        n = len(self.started)
        copy = pltpu.make_async_remote_copy(
            src_ref=src, dst_ref=dst, send_sem=self.send_sem.at[n], recv_sem=self.recv_sem.at[n],
            device_id=to, device_id_type=MESH,
        )
        copy.start()
        self.started.append(copy)
        return copy

    def finish(self):
        for copy in self.started:
            copy.wait_send()


GATHER_COPIES = 3 + 6 + 2 * (4 * 2 + 4 + 7 * 2 + 4 * 2) + 32 + 10


def gather_kernel(q_ref, kv_ref, doc_ref, heads_ref, length_ref, kvx_ref, notes_ref, qx_ref, note, send_sem, recv_sem):
    x, y, z, core = place()
    col = lax.axis_index("kvcol")
    row = lax.axis_index("qrow")
    nx = [(x + 1) % 4, (x + 3) % 4]
    nz = [(z + 1) % 4, (z + 3) % 4]
    ys = [(y + k) % 4 for k in range(4)]
    beside = device(x, y, z, 1 - core)
    legs = {0: [device(v, y, z, core) for v in nx], 1: [device(x, y, v, core) for v in nz]}
    xs = [device((x + k) % 4, y, z, core) for k in (1, 3, 2)]
    zs = [device(x, y, (z + k) % 4, core) for k in (1, 3, 2)]
    greet(xs + zs + [beside] + [device(x, ys[k], z, core) for k in (1, 2, 3)])

    copies = Copies(send_sem, recv_sem)

    def part(half, bx, bz, which):
        return kvx_ref.at[half, row_of(bx, bz, core), which, bz % 2]

    def head_slice(ref, index, width):
        return ref.at[:, pl.ds(pl.multiple_of(index * width, width), width)]

    every = pl.ds(0, 4)
    own = [head_slice(kv_ref.at[h], y, HEAD) for h in (0, 1)]
    first = {}
    for h in (0, 1):
        for way in (0, 1):
            first[h, 0, way] = copies.send(own[h], part(h, x, z, y), legs[h][way])
    second = {}
    for h in (0, 1):
        for way in (0, 1):
            second[h, 0, way] = [copies.send(own[h], part(h, x, z, y), legs[1 - h][way])]
    across = {}
    for k in (1, 3, 2):
        src = kv_ref.at[:, :, pl.ds(pl.multiple_of(ys[k] * HEAD, HEAD), HEAD)]
        across[k] = copies.send(src, kvx_ref.at[:, row, y, z % 2], device(x, ys[k], z, core))
    for v in range(KV_HEADS):
        @pl.when(y == v)
        def _():
            for h in (0, 1):
                kvx_ref[h, row, v, z % 2] = kv_ref[h, :, v * HEAD:(v + 1) * HEAD]
            for layer in range(LAYERS):
                at = (layer * KV_HEADS + v) * GROUP * HEAD
                qx_ref[v, layer] = q_ref[:, at:at + GROUP * HEAD]

    lane = lax.broadcasted_iota(jnp.int32, (1, TOK), 1)
    lengths = jnp.zeros((1, TOK), jnp.int32)
    for h in range(KV_HEADS):
        k = kv_ref[0, :, h * HEAD:(h + 1) * HEAD].astype(jnp.float32)
        most = jnp.max(jnp.sum(k * k, axis=1, keepdims=True), axis=0, keepdims=True)
        lengths = jnp.where(lane == h, most.astype(jnp.int32) + 1, lengths)
    note[0:1, :] = doc_ref[...]
    note[1:2, :] = lengths
    zh, zl = z // 2, z % 2
    notes_ref[x, zh, core, y, zl] = note[...]
    told = [copies.send(note, notes_ref.at[x, zh, core, y, zl], device(x, ys[k], z, core)) for k in (1, 3, 2)]
    for k in (1, 3, 2):
        across[k].wait_recv()
        for h in (0, 1):
            ref = part(h, x, z, (y + 4 - k) % 4)
            for way in (0, 1):
                first[h, k, way] = copies.send(ref, ref, legs[h][way])
        for h in (0, 1):
            ref = part(h, x, z, (y + 4 - k) % 4)
            for way in (0, 1):
                second[h, 0, way].append(copies.send(ref, ref, legs[1 - h][way]))

    width = GROUP * HEAD
    asked = []
    for k in (1, 3, 2):
        for layer in range(LAYERS):
            asked.append(copies.send(
                head_slice(q_ref, layer * KV_HEADS + ys[k], width), qx_ref.at[y, layer], device(x, ys[k], z, core)))
    def tell(places, to):
        for c in told:
            c.wait_recv()
        ref = notes_ref.at[places]
        return [copies.send(ref, ref, d) for d in to]

    told = tell((x, zh, core, every, zl), xs)

    given = []

    def share(half, bx, bz):
        ref = part(half, bx, bz, every)
        given.append(copies.send(ref, ref, beside))

    def onward(half, step, bx, bz):
        ref = part(half, bx, bz, every)
        for way in (0, 1):
            second[half, step, way] = [copies.send(ref, ref, legs[1 - half][way])]
        share(half, bx, bz)

    def came(half, way):
        if half == 0:
            return (nx[1 - way], z)
        return (x, nz[1 - way])

    for h in (0, 1):
        share(h, x, z)
    further = {}
    for k in (0, 1, 3, 2):
        way = 0 if k < 2 else 1
        for h in (0, 1):
            first[h, k, way].wait_recv()
            ref = part(h, *came(h, way), (y + 4 - k) % 4)
            further[h, k] = copies.send(ref, ref, legs[h][way])
    for way in (0, 1):
        for k in ((2, 3), (0, 1))[way]:
            for h in (0, 1):
                first[h, k, way].wait_recv()
        for h in (0, 1):
            onward(h, 1 + way, *came(h, way))
    told = tell((every, zh, core, every, zl), zs)
    for h in (0, 1):
        for k in range(4):
            further[h, k].wait_recv()
        opposite = ((x + 2) % 4, z) if h == 0 else (x, (z + 2) % 4)
        onward(h, 3, *opposite)

    def row_block(half, step):
        if half == 0:
            return [x, nx[1], nx[0], (x + 2) % 4][step]
        return [z, nz[1], nz[0], (z + 2) % 4][step]

    last = {}
    for step in range(4):
        if step == 2:
            told = tell((every, slice(None), core), [beside])
        for h in (0, 1):
            for way in (0, 1):
                for c in second[h, step, way]:
                    c.wait_recv()
                b = row_block(h, step)
                bx, bz = (b, nz[1 - way]) if h == 0 else (nx[1 - way], b)
                ref = part(h, bx, bz, pl.ds(2 * way, 2))
                last[h, step, way] = copies.send(ref, ref, legs[1 - h][way])
                share(h, bx, bz)
    for c in asked:
        c.wait_recv()
    length = jnp.zeros((TOK, 1), jnp.float32)
    for t in range(4):
        for g in range(LAYERS * GROUP):
            head = qx_ref[t, g // GROUP, :, (g % GROUP) * HEAD:(g % GROUP + 1) * HEAD]
            heads_ref[t, g * TOK:(g + 1) * TOK, :] = head
            head = head.astype(jnp.float32)
            length = jnp.maximum(length, jnp.sum(head * head, axis=1, keepdims=True))
    length_ref[...] = jnp.broadcast_to(jnp.max(length, axis=0, keepdims=True), (1, TOK))
    for step in range(4):
        for h in (0, 1):
            for way in (0, 1):
                last[h, step, way].wait_recv()
            b = row_block(h, step)
            share(h, *((b, (z + 2) % 4) if h == 0 else ((x + 2) % 4, b)))
    for c in given + told:
        c.wait_recv()
    copies.finish()


def gather(q, kv, document):
    return pl.pallas_call(
        gather_kernel,
        out_shape=[
            jax.ShapeDtypeStruct((KV_HEADS, LAYERS * GROUP * TOK, HEAD), q.dtype),
            jax.ShapeDtypeStruct((1, TOK), jnp.float32),
            jax.ShapeDtypeStruct((2, 16, 4, 2, TOK, HEAD), kv.dtype),
            jax.ShapeDtypeStruct((4, 2, 2, 4, 2, 2, TOK), jnp.int32),
        ],
        in_specs=[pl.BlockSpec(memory_space=pltpu.VMEM)] * 3,
        out_specs=[pl.BlockSpec(memory_space=pltpu.VMEM)] * 4,
        scratch_shapes=[
            pltpu.VMEM((KV_HEADS, LAYERS, TOK, GROUP * HEAD), q.dtype),
            pltpu.VMEM((2, TOK), jnp.int32),
            pltpu.SemaphoreType.DMA((GATHER_COPIES,)),
            pltpu.SemaphoreType.DMA((GATHER_COPIES,)),
        ],
        compiler_params=pltpu.CompilerParams(collective_id=0, has_side_effects=True, vmem_limit_bytes=16 * 2**20),
    )(q, kv, document)


def return_kernel(o_ref, out_ref, relay, send_sem, recv_sem):
    x, y, z, core = place()
    ys = [(y + k) % 4 for k in range(4)]
    to = [device(x, ys[k], z, core) for k in range(4)]
    greet(to[1:])
    copies = Copies(send_sem, recv_sem)
    width = GROUP * HEAD

    def span(owner, layer):
        return out_ref.at[:, pl.ds(pl.multiple_of((layer * KV_HEADS + owner) * width, width), width)]

    hops = (to[1], to[3])
    handed = [copies.send(o_ref.at[ys[2], layer], relay.at[layer], hops[layer]) for layer in range(LAYERS)]
    direct = [copies.send(o_ref.at[ys[k], layer], span(y, layer), to[k]) for layer in range(LAYERS) for k in (1, 3)]
    for v in range(KV_HEADS):
        @pl.when(y == v)
        def _():
            for layer in range(LAYERS):
                at = (layer * KV_HEADS + v) * width
                out_ref[:, at:at + width] = o_ref[v, layer]
    onward = []
    for layer in range(LAYERS):
        handed[layer].wait_recv()
        onward.append(copies.send(relay.at[layer], span(ys[3 if layer == 0 else 1], layer), hops[layer]))
    for c in direct + onward:
        c.wait_recv()
    copies.finish()


def give_back(o):
    return pl.pallas_call(
        return_kernel,
        out_shape=jax.ShapeDtypeStruct((TOK, LAYERS * Q_HEADS * HEAD), o.dtype),
        in_specs=[pl.BlockSpec(memory_space=pltpu.VMEM)],
        out_specs=pl.BlockSpec(memory_space=pltpu.VMEM),
        scratch_shapes=[
            pltpu.VMEM((LAYERS, TOK, GROUP * HEAD), o.dtype),
            pltpu.SemaphoreType.DMA((8,)),
            pltpu.SemaphoreType.DMA((8,)),
        ],
        compiler_params=pltpu.CompilerParams(collective_id=1, has_side_effects=True, vmem_limit_bytes=16 * 2**20),
    )(o)


SCALE = 1.4426950408889634 * HEAD ** -0.5
NEG=-1e30
BIG = 100.0
KB = 512
KI = 1024

def attend_kernel(kb, ki, chunk_ref, notes_ref, length_ref, q_ref, kv_ref, o_ref, acc, top):
    tiles = q_ref.shape[0]
    heads = LAYERS*GROUP
    rows = heads*TOK

    labels = notes_ref[:, 0, :]
    head = chunk_ref[tiles]
    lane = lax.broadcasted_iota(jnp.int32, (1, TOK), 1)
    longest = jnp.max(jnp.where(lane == head, jnp.max(notes_ref[:, 1, :], axis=0, keepdims=True), 0)).astype(jnp.float32)
    bounds = []
    for t in range(tiles):
        chunk = chunk_ref[t]
        mine = notes_ref[chunk, 0:1, :]
        low = jnp.min(mine, axis=1, keepdims=True)
        bounds.append((chunk, jnp.sum((labels < low).astype(jnp.int32))))
    small = jnp.max(length_ref[...])*longest <= (BIG/SCALE)**2

    def tile(t):
        chunk, first = bounds[t]
        end = (chunk + 1)*TOK
        mine = notes_ref[chunk, 0:1, :]
        span = jnp.maximum(end - first - kb, 0)
        full = span//ki
        edges = 1 + (span - full*ki + kb - 1)//kb
        below = jnp.transpose(jnp.broadcast_to(mine, (TOK, TOK))) < mine
        inside = end - TOK + jnp.sum(below.astype(jnp.int32), axis=0, keepdims=True)
        ahead = mine == jnp.min(mine, axis=1, keepdims=True)
        lowest = jnp.where(ahead, first, inside)
        ahead = jnp.concatenate([ahead]*heads, axis=1)
        place = end - TOK + lax.broadcasted_iota(jnp.int32, (1, TOK), 1)

        def edge(n):
            stop = end - jnp.where(n == 0, 0, n*kb + full*ki)
            start = jnp.maximum(stop - kb, 0)
            key = start + lax.broadcasted_iota(jnp.int32, (kb, TOK), 0)
            return start, (key >= lowest) & (key <= jnp.minimum(place, stop - 1))

        def block(start, size):
            at = pl.ds(pl.multiple_of(start, TOK), size)
            v = jnp.concatenate([jnp.transpose(kv_ref[1, at, :]), jnp.ones((16, size), kv_ref.dtype)], axis=0)
            return kv_ref[0, at, :], v

        def inner(n):
            return end - kb - (n + 1)*ki

        def dot_q(k, r):
            return lax.dot_general(k, q_ref[t, r, :], (((1,), (1,)), ((), ())), preferred_element_type=jnp.float32)*SCALE

        def quick(n, _):
            k, v = block(inner(n), ki)
            p = jnp.exp2(dot_q(k, pl.ds(0, rows)))
            acc[t] += jnp.where(ahead, jnp.dot(v, p.astype(v.dtype), preferred_element_type=jnp.float32), 0.0)

        def quick_edge(n):
            start, mask = edge(n)
            k, v = block(start, kb)
            p = jnp.exp2(dot_q(k, pl.ds(0, rows)))
            p = jnp.where(jnp.concatenate([mask]*heads, axis=1), p, 0.0)
            return jnp.dot(v, p.astype(v.dtype), preferred_element_type=jnp.float32)

        def quick_more(n, _):
            acc[t] += quick_edge(n)

        def careful(k, v, mask):
            for g in range(heads):
                r = pl.ds(g*TOK, TOK)
                s = dot_q(k, r)
                if mask is not None:
                    s = jnp.where(mask, s, NEG)
                old = top[0:1, r]
                new = jnp.maximum(old, jnp.max(s, axis=0, keepdims=True))
                top[0:1, r] = new
                p = jnp.exp2(s - new)
                if mask is not None:
                    p = jnp.where(mask, p, 0.0)
                acc[t, :, r] = acc[t, :, r]*jnp.exp2(old - new) + jnp.dot(v, p.astype(v.dtype), preferred_element_type=jnp.float32)

        def careful_full(n, _):
            careful(*block(inner(n), ki), None)

        def careful_edge(n, _):
            start, mask = edge(n)
            careful(*block(start, kb), mask)

        def begin():
            acc[t] = quick_edge(0)

        def proceed():
            lax.fori_loop(0, full, quick, None)
            lax.fori_loop(1, edges, quick_more, None)

        def with_care():
            acc[t] = jnp.zeros(acc.shape[1:], acc.dtype)
            top[...] = jnp.full_like(top, NEG)
            lax.fori_loop(0, full, careful_full, None)
            acc[t] = jnp.where(ahead, acc[t], 0.0)
            top[...] = jnp.where(ahead, top[...], NEG)
            lax.fori_loop(0, edges, careful_edge, None)

        return begin, proceed, with_care

    steps = [tile(t) for t in range(tiles)]

    @pl.when(small)
    def _():
        for begin, _, _ in steps:
            begin()
        for _, proceed, _ in steps:
            proceed()

    @pl.when(jnp.logical_not(small))
    def _():
        for _, _, with_care in steps:
            with_care()

    for t in range(tiles):
        for g in range(heads):
            r = pl.ds(g*TOK, TOK)
            o = acc[t, :HEAD, r]/acc[t, HEAD:HEAD + 1, r]
            h = g % GROUP
            o_ref[t, g//GROUP, :, h*HEAD:(h + 1)*HEAD] = jnp.transpose(o).astype(o_ref.dtype)


def attend(chunk, notes, length, q, kv, kb=KB, ki=KI):
    tiles, rows, _ = q.shape
    shape = (tiles, LAYERS, TOK, GROUP*HEAD)
    vmem = pl.BlockSpec(memory_space=pltpu.VMEM)
    return pl.pallas_call(
        functools.partial(attend_kernel, kb, ki),
        out_shape=jax.ShapeDtypeStruct(shape, q.dtype),
        in_specs=[pl.BlockSpec(memory_space=pltpu.SMEM)] + [vmem]*4,
        out_specs=vmem,
        scratch_shapes=[
            pltpu.VMEM((tiles, HEAD + 16, rows), jnp.float32),
            pltpu.VMEM((8, rows), jnp.float32),
        ],
        compiler_params=pltpu.CompilerParams(vmem_limit_bytes=40*2**20),
    )(chunk, notes, length, q, kv)


def shards(queries, shared_kv, document):
    row, col = lax.axis_index("qrow"), lax.axis_index("kvcol")
    heads, length, kvx, notes = gather(queries[0], shared_kv[:, 0], document[None])
    tiles = [t * 32 + (col % 2) * 16 + row for t in range(4)]
    chunk = jnp.stack(tiles + [col // 2]).astype(jnp.int32)
    o = attend(chunk, notes.reshape(-1, 2, TOK), length, heads, kvx.reshape(2, -1, HEAD))
    out = give_back(o)
    return out.reshape(queries.shape)


def solution(mesh):
    placed = (P("kvcol", "qrow", None), P(None, "qrow", "kvcol", None), P(("qrow", "kvcol")))
    return jax.shard_map(
        shards, mesh=mesh, in_specs=placed, out_specs=P("kvcol", "qrow", None), check_vma=False
    )
```

```python
import functools
import jax
import jax.numpy as jnp
from jax import lax
from jax.experimental import pallas as pl
from jax.experimental.pallas import tpu as pltpu
from jax.sharding import PartitionSpec as P

HEAD = 128
Q_HEADS = 16
KV_HEADS = 4
LAYERS = 2
GROUP = Q_HEADS // KV_HEADS
TOK = 128
MESH = pl.DeviceIdType.MESH


def place():
    row, col = lax.axis_index("qrow"), lax.axis_index("kvcol")
    return row // 4, col // 2, ((row // 2) % 2) * 2 + col % 2, row % 2


def row_of(x, z, core):
    return (x * 2 + z // 2) * 2 + core


def device(x, y, z, core):
    return (row_of(x, z, core), y * 2 + z % 2)


def greet(devices):
    barrier = pltpu.get_barrier_semaphore()
    for d in devices:
        pl.semaphore_signal(barrier, inc=1, device_id=d, device_id_type=MESH)
    pl.semaphore_wait(barrier, len(devices))


class Copies:
    def __init__(self, send_sem, recv_sem):
        self.send_sem, self.recv_sem, self.started = send_sem, recv_sem, []

    def send(self, src, dst, to):
        n = len(self.started)
        copy = pltpu.make_async_remote_copy(
            src_ref=src, dst_ref=dst, send_sem=self.send_sem.at[n], recv_sem=self.recv_sem.at[n],
            device_id=to, device_id_type=MESH,
        )
        copy.start()
        self.started.append(copy)
        return copy

    def finish(self):
        for copy in self.started:
            copy.wait_send()


GATHER_COPIES = 3 + 6 + 2 * (4 * 2 + 4 + 7 * 2 + 4 * 2) + 32 + 10


def gather_kernel(q_ref, kv_ref, doc_ref, heads_ref, length_ref, kvx_ref, notes_ref, qx_ref, note, send_sem, recv_sem):
    x, y, z, core = place()
    col = lax.axis_index("kvcol")
    row = lax.axis_index("qrow")
    nx = [(x + 1) % 4, (x + 3) % 4]
    nz = [(z + 1) % 4, (z + 3) % 4]
    ys = [(y + k) % 4 for k in range(4)]
    beside = device(x, y, z, 1 - core)
    legs = {0: [device(v, y, z, core) for v in nx], 1: [device(x, y, v, core) for v in nz]}
    xs = [device((x + k) % 4, y, z, core) for k in (1, 3, 2)]
    zs = [device(x, y, (z + k) % 4, core) for k in (1, 3, 2)]
    greet(xs + zs + [beside] + [device(x, ys[k], z, core) for k in (1, 2, 3)])

    copies = Copies(send_sem, recv_sem)

    def part(half, bx, bz, which):
        return kvx_ref.at[half, row_of(bx, bz, core), which, bz % 2]

    def head_slice(ref, index, width):
        return ref.at[:, pl.ds(pl.multiple_of(index * width, width), width)]

    every = pl.ds(0, 4)
    own = [head_slice(kv_ref.at[h], y, HEAD) for h in (0, 1)]
    first = {}
    for h in (0, 1):
        for way in (0, 1):
            first[h, 0, way] = copies.send(own[h], part(h, x, z, y), legs[h][way])
    second = {}
    for h in (0, 1):
        for way in (0, 1):
            second[h, 0, way] = [copies.send(own[h], part(h, x, z, y), legs[1 - h][way])]
    across = {}
    for k in (1, 3, 2):
        src = kv_ref.at[:, :, pl.ds(pl.multiple_of(ys[k] * HEAD, HEAD), HEAD)]
        across[k] = copies.send(src, kvx_ref.at[:, row, y, z % 2], device(x, ys[k], z, core))
    for v in range(KV_HEADS):
        @pl.when(y == v)
        def _():
            for h in (0, 1):
                kvx_ref[h, row, v, z % 2] = kv_ref[h, :, v * HEAD:(v + 1) * HEAD]
            for layer in range(LAYERS):
                at = (layer * KV_HEADS + v) * GROUP * HEAD
                qx_ref[v, layer] = q_ref[:, at:at + GROUP * HEAD]

    lane = lax.broadcasted_iota(jnp.int32, (1, TOK), 1)
    lengths = jnp.zeros((1, TOK), jnp.int32)
    for h in range(KV_HEADS):
        k = kv_ref[0, :, h * HEAD:(h + 1) * HEAD].astype(jnp.float32)
        most = jnp.max(jnp.sum(k * k, axis=1, keepdims=True), axis=0, keepdims=True)
        lengths = jnp.where(lane == h, most.astype(jnp.int32) + 1, lengths)
    note[0:1, :] = doc_ref[...]
    note[1:2, :] = lengths
    zh, zl = z // 2, z % 2
    notes_ref[x, zh, core, y, zl] = note[...]
    told = [copies.send(note, notes_ref.at[x, zh, core, y, zl], device(x, ys[k], z, core)) for k in (1, 3, 2)]
    for k in (1, 3, 2):
        across[k].wait_recv()
        for h in (0, 1):
            ref = part(h, x, z, (y + 4 - k) % 4)
            for way in (0, 1):
                first[h, k, way] = copies.send(ref, ref, legs[h][way])
        for h in (0, 1):
            ref = part(h, x, z, (y + 4 - k) % 4)
            for way in (0, 1):
                second[h, 0, way].append(copies.send(ref, ref, legs[1 - h][way]))

    width = GROUP * HEAD
    asked = []
    for k in (1, 3, 2):
        for layer in range(LAYERS):
            asked.append(copies.send(
                head_slice(q_ref, layer * KV_HEADS + ys[k], width), qx_ref.at[y, layer], device(x, ys[k], z, core)))
    def tell(places, to):
        for c in told:
            c.wait_recv()
        ref = notes_ref.at[places]
        return [copies.send(ref, ref, d) for d in to]

    told = tell((x, zh, core, every, zl), xs)

    given = []

    def share(half, bx, bz):
        ref = part(half, bx, bz, every)
        given.append(copies.send(ref, ref, beside))

    def onward(half, step, bx, bz):
        ref = part(half, bx, bz, every)
        for way in (0, 1):
            second[half, step, way] = [copies.send(ref, ref, legs[1 - half][way])]
        share(half, bx, bz)

    def came(half, way):
        if half == 0:
            return (nx[1 - way], z)
        return (x, nz[1 - way])

    for h in (0, 1):
        share(h, x, z)
    further = {}
    for k in (0, 1, 3, 2):
        way = 0 if k < 2 else 1
        for h in (0, 1):
            first[h, k, way].wait_recv()
            ref = part(h, *came(h, way), (y + 4 - k) % 4)
            further[h, k] = copies.send(ref, ref, legs[h][way])
    for way in (0, 1):
        for k in ((2, 3), (0, 1))[way]:
            for h in (0, 1):
                first[h, k, way].wait_recv()
        for h in (0, 1):
            onward(h, 1 + way, *came(h, way))
    told = tell((every, zh, core, every, zl), zs)
    for h in (0, 1):
        for k in range(4):
            further[h, k].wait_recv()
        opposite = ((x + 2) % 4, z) if h == 0 else (x, (z + 2) % 4)
        onward(h, 3, *opposite)

    def row_block(half, step):
        if half == 0:
            return [x, nx[1], nx[0], (x + 2) % 4][step]
        return [z, nz[1], nz[0], (z + 2) % 4][step]

    last = {}
    for step in range(4):
        if step == 2:
            told = tell((every, slice(None), core), [beside])
        for h in (0, 1):
            for way in (0, 1):
                for c in second[h, step, way]:
                    c.wait_recv()
                b = row_block(h, step)
                bx, bz = (b, nz[1 - way]) if h == 0 else (nx[1 - way], b)
                ref = part(h, bx, bz, pl.ds(2 * way, 2))
                last[h, step, way] = copies.send(ref, ref, legs[1 - h][way])
                share(h, bx, bz)
    for c in asked:
        c.wait_recv()
    length = jnp.zeros((TOK, 1), jnp.float32)
    for t in range(4):
        for g in range(LAYERS * GROUP):
            head = qx_ref[t, g // GROUP, :, (g % GROUP) * HEAD:(g % GROUP + 1) * HEAD]
            heads_ref[t, g * TOK:(g + 1) * TOK, :] = head
            head = head.astype(jnp.float32)
            length = jnp.maximum(length, jnp.sum(head * head, axis=1, keepdims=True))
    length_ref[...] = jnp.broadcast_to(jnp.max(length, axis=0, keepdims=True), (1, TOK))
    for step in range(4):
        for h in (0, 1):
            for way in (0, 1):
                last[h, step, way].wait_recv()
            b = row_block(h, step)
            share(h, *((b, (z + 2) % 4) if h == 0 else ((x + 2) % 4, b)))
    for c in given + told:
        c.wait_recv()
    copies.finish()


def gather(q, kv, document):
    return pl.pallas_call(
        gather_kernel,
        out_shape=[
            jax.ShapeDtypeStruct((KV_HEADS, LAYERS * GROUP * TOK, HEAD), q.dtype),
            jax.ShapeDtypeStruct((1, TOK), jnp.float32),
            jax.ShapeDtypeStruct((2, 16, 4, 2, TOK, HEAD), kv.dtype),
            jax.ShapeDtypeStruct((4, 2, 2, 4, 2, 2, TOK), jnp.int32),
        ],
        in_specs=[pl.BlockSpec(memory_space=pltpu.VMEM)] * 3,
        out_specs=[pl.BlockSpec(memory_space=pltpu.VMEM)] * 4,
        scratch_shapes=[
            pltpu.VMEM((KV_HEADS, LAYERS, TOK, GROUP * HEAD), q.dtype),
            pltpu.VMEM((2, TOK), jnp.int32),
            pltpu.SemaphoreType.DMA((GATHER_COPIES,)),
            pltpu.SemaphoreType.DMA((GATHER_COPIES,)),
        ],
        compiler_params=pltpu.CompilerParams(collective_id=0, has_side_effects=True, vmem_limit_bytes=16 * 2**20),
    )(q, kv, document)


def return_kernel(o_ref, out_ref, relay, send_sem, recv_sem):
    x, y, z, core = place()
    ys = [(y + k) % 4 for k in range(4)]
    to = [device(x, ys[k], z, core) for k in range(4)]
    greet(to[1:])
    copies = Copies(send_sem, recv_sem)
    width = GROUP * HEAD

    def span(owner, layer):
        return out_ref.at[:, pl.ds(pl.multiple_of((layer * KV_HEADS + owner) * width, width), width)]

    hops = (to[1], to[3])
    handed = [copies.send(o_ref.at[ys[2], layer], relay.at[layer], hops[layer]) for layer in range(LAYERS)]
    direct = [copies.send(o_ref.at[ys[k], 0], span(y, 0), to[k]) for k in (1, 3)]
    for v in range(KV_HEADS):
        @pl.when(y == v)
        def _():
            for layer in range(LAYERS):
                at = (layer * KV_HEADS + v) * width
                out_ref[:, at:at + width] = o_ref[v, layer]
    onward = []
    for layer in range(LAYERS):
        handed[layer].wait_recv()
        onward.append(copies.send(relay.at[layer], span(ys[3 if layer == 0 else 1], layer), hops[layer]))
    direct += [copies.send(o_ref.at[ys[k], 1], span(y, 1), to[k]) for k in (1, 3)]
    for c in direct + onward:
        c.wait_recv()
    copies.finish()


def give_back(o):
    return pl.pallas_call(
        return_kernel,
        out_shape=jax.ShapeDtypeStruct((TOK, LAYERS * Q_HEADS * HEAD), o.dtype),
        in_specs=[pl.BlockSpec(memory_space=pltpu.VMEM)],
        out_specs=pl.BlockSpec(memory_space=pltpu.VMEM),
        scratch_shapes=[
            pltpu.VMEM((LAYERS, TOK, GROUP * HEAD), o.dtype),
            pltpu.SemaphoreType.DMA((8,)),
            pltpu.SemaphoreType.DMA((8,)),
        ],
        compiler_params=pltpu.CompilerParams(collective_id=1, has_side_effects=True, vmem_limit_bytes=16 * 2**20),
    )(o)


SCALE = 1.4426950408889634 * HEAD ** -0.5
NEG=-1e30
BIG = 100.0
KB = 512
KI = 1024

def attend_kernel(kb, ki, chunk_ref, notes_ref, length_ref, q_ref, kv_ref, o_ref, acc, top):
    tiles = q_ref.shape[0]
    heads = LAYERS*GROUP
    rows = heads*TOK

    labels = notes_ref[:, 0, :]
    head = chunk_ref[tiles]
    lane = lax.broadcasted_iota(jnp.int32, (1, TOK), 1)
    longest = jnp.max(jnp.where(lane == head, jnp.max(notes_ref[:, 1, :], axis=0, keepdims=True), 0)).astype(jnp.float32)
    bounds = []
    for t in range(tiles):
        chunk = chunk_ref[t]
        mine = notes_ref[chunk, 0:1, :]
        low = jnp.min(mine, axis=1, keepdims=True)
        bounds.append((chunk, jnp.sum((labels < low).astype(jnp.int32))))
    small = jnp.max(length_ref[...])*longest <= (BIG/SCALE)**2

    def tile(t):
        chunk, first = bounds[t]
        end = (chunk + 1)*TOK
        mine = notes_ref[chunk, 0:1, :]
        span = jnp.maximum(end - first - kb, 0)
        full = span//ki
        edges = 1 + (span - full*ki + kb - 1)//kb
        below = jnp.transpose(jnp.broadcast_to(mine, (TOK, TOK))) < mine
        inside = end - TOK + jnp.sum(below.astype(jnp.int32), axis=0, keepdims=True)
        ahead = mine == jnp.min(mine, axis=1, keepdims=True)
        lowest = jnp.where(ahead, first, inside)
        ahead = jnp.concatenate([ahead]*heads, axis=1)
        place = end - TOK + lax.broadcasted_iota(jnp.int32, (1, TOK), 1)

        def edge(n):
            stop = end - jnp.where(n == 0, 0, n*kb + full*ki)
            start = jnp.maximum(stop - kb, 0)
            key = start + lax.broadcasted_iota(jnp.int32, (kb, TOK), 0)
            return start, (key >= lowest) & (key <= jnp.minimum(place, stop - 1))

        def block(start, size):
            at = pl.ds(pl.multiple_of(start, TOK), size)
            v = jnp.concatenate([jnp.transpose(kv_ref[1, at, :]), jnp.ones((16, size), kv_ref.dtype)], axis=0)
            return kv_ref[0, at, :], v

        def inner(n):
            return end - kb - (n + 1)*ki

        def dot_q(k, r):
            return lax.dot_general(k, q_ref[t, r, :], (((1,), (1,)), ((), ())), preferred_element_type=jnp.float32)*SCALE

        def quick(n, _):
            k, v = block(inner(n), ki)
            p = jnp.exp2(dot_q(k, pl.ds(0, rows)))
            acc[t] += jnp.where(ahead, jnp.dot(v, p.astype(v.dtype), preferred_element_type=jnp.float32), 0.0)

        def quick_edge(n):
            start, mask = edge(n)
            k, v = block(start, kb)
            p = jnp.exp2(dot_q(k, pl.ds(0, rows)))
            p = jnp.where(jnp.concatenate([mask]*heads, axis=1), p, 0.0)
            return jnp.dot(v, p.astype(v.dtype), preferred_element_type=jnp.float32)

        def quick_more(n, _):
            acc[t] += quick_edge(n)

        def careful(k, v, mask):
            for g in range(heads):
                r = pl.ds(g*TOK, TOK)
                s = dot_q(k, r)
                if mask is not None:
                    s = jnp.where(mask, s, NEG)
                old = top[0:1, r]
                new = jnp.maximum(old, jnp.max(s, axis=0, keepdims=True))
                top[0:1, r] = new
                p = jnp.exp2(s - new)
                if mask is not None:
                    p = jnp.where(mask, p, 0.0)
                acc[t, :, r] = acc[t, :, r]*jnp.exp2(old - new) + jnp.dot(v, p.astype(v.dtype), preferred_element_type=jnp.float32)

        def careful_full(n, _):
            careful(*block(inner(n), ki), None)

        def careful_edge(n, _):
            start, mask = edge(n)
            careful(*block(start, kb), mask)

        def begin():
            acc[t] = quick_edge(0)

        def proceed():
            lax.fori_loop(0, full, quick, None)
            lax.fori_loop(1, edges, quick_more, None)

        def with_care():
            acc[t] = jnp.zeros(acc.shape[1:], acc.dtype)
            top[...] = jnp.full_like(top, NEG)
            lax.fori_loop(0, full, careful_full, None)
            acc[t] = jnp.where(ahead, acc[t], 0.0)
            top[...] = jnp.where(ahead, top[...], NEG)
            lax.fori_loop(0, edges, careful_edge, None)

        return begin, proceed, with_care

    steps = [tile(t) for t in range(tiles)]

    @pl.when(small)
    def _():
        for begin, _, _ in steps:
            begin()
        for _, proceed, _ in steps:
            proceed()

    @pl.when(jnp.logical_not(small))
    def _():
        for _, _, with_care in steps:
            with_care()

    for t in range(tiles):
        for g in range(heads):
            r = pl.ds(g*TOK, TOK)
            o = acc[t, :HEAD, r]/acc[t, HEAD:HEAD + 1, r]
            h = g % GROUP
            o_ref[t, g//GROUP, :, h*HEAD:(h + 1)*HEAD] = jnp.transpose(o).astype(o_ref.dtype)


def attend(chunk, notes, length, q, kv, kb=KB, ki=KI):
    tiles, rows, _ = q.shape
    shape = (tiles, LAYERS, TOK, GROUP*HEAD)
    vmem = pl.BlockSpec(memory_space=pltpu.VMEM)
    return pl.pallas_call(
        functools.partial(attend_kernel, kb, ki),
        out_shape=jax.ShapeDtypeStruct(shape, q.dtype),
        in_specs=[pl.BlockSpec(memory_space=pltpu.SMEM)] + [vmem]*4,
        out_specs=vmem,
        scratch_shapes=[
            pltpu.VMEM((tiles, HEAD + 16, rows), jnp.float32),
            pltpu.VMEM((8, rows), jnp.float32),
        ],
        compiler_params=pltpu.CompilerParams(vmem_limit_bytes=40*2**20),
    )(chunk, notes, length, q, kv)


def shards(queries, shared_kv, document):
    row, col = lax.axis_index("qrow"), lax.axis_index("kvcol")
    heads, length, kvx, notes = gather(queries[0], shared_kv[:, 0], document[None])
    tiles = [t * 32 + (col % 2) * 16 + row for t in range(4)]
    chunk = jnp.stack(tiles + [col // 2]).astype(jnp.int32)
    o = attend(chunk, notes.reshape(-1, 2, TOK), length, heads, kvx.reshape(2, -1, HEAD))
    out = give_back(o)
    return out.reshape(queries.shape)


def solution(mesh):
    placed = (P("kvcol", "qrow", None), P(None, "qrow", "kvcol", None), P(("qrow", "kvcol")))
    return jax.shard_map(
        shards, mesh=mesh, in_specs=placed, out_specs=P("kvcol", "qrow", None), check_vma=False
    )
```
